32 devices in a mesh: tx: 4 (over y, core), ty: 8 (over z, x).
Axes of the slice: x: 2, y: 2, z: 4, core: 2. Of those that a mesh axis runs over, the one named last changes fastest.
Arguments:
- increment: float32 [32, 640, 3072], P(None, 'ty', 'tx'), may hold values from -6 to 6
- vert_rate: float32 [2, 16], replicated, may hold values from 0.05 to 0.8
- zonal_rate: float32 [16, 32], replicated, may hold values from 0.003 to 0.12
- merid_rate: float32 [16, 32], replicated, may hold values from 0.02 to 0.12
- lat_band: int32 [640], replicated, may hold values from 0 to 15, never falling along the last dimension, each value on 1 to 80 neighbouring positions
- slab_owner: int32 [32], replicated, may hold values from 0 to 3, as said below
Outputs:
- covariance_product: float32 [32, 640, 3072], P(None, 'ty', 'tx')
- filtered_slabs: float32 [64, 640, 3072], P('tx', 'ty')
The draws below stay inside these ranges and needn't reach their ends.
Inputs may be any that keep to these rules, and one draw needn't show every extreme that they name: lat_band never falls along y and every band appears. `slab_owner`: each index of tx owns at most 16 slabs, and some index owns exactly 16.
All inputs are finite; a program needn't handle non-finite values.
Results may differ from the reference program's by a relative error of at most 0.0003.
Values sent between devices are 32-bit elements; how exact they have to be, the bound alone decides.
No kernel may reach another device: no remote copies, remote signals or barrier semaphores. Data moves between devices by JAX's collectives and lax.ppermute only.
A program may use at most 128 MiB of HBM per device.

```python
import math
import jax
import jax.numpy as jnp
import numpy as np
from jax import lax

NX = 3072
NY = 640
LEV = 16
VAR = 2
NBANDS = 16
SLABS = 32
CAP = 16
N_TX = 4


def draw_slab_owner(key, part):
    groups = 2 * SLABS // CAP
    order = jax.random.permutation(jax.random.fold_in(key, 11), SLABS)
    heavy = jax.random.randint(jax.random.fold_in(key, 12), (), 0, groups)
    ranks = jnp.arange(SLABS, dtype=jnp.int32)
    others = (heavy + 1 + (ranks - CAP) % (groups - 1)) % groups
    by_rank = jnp.where(ranks < CAP, heavy, others).astype(jnp.int32)
    return jnp.zeros((SLABS,), jnp.int32).at[order].set(by_rank)


def draw_zonal_rate(key, part):
    shape = (NBANDS, SLABS)
    rates = jnp.exp(jax.random.uniform(jax.random.fold_in(key, 24), shape, jnp.float32, math.log(0.003), math.log(0.12)))
    return jnp.clip(rates, 0.003, 0.12).astype(jnp.float32)


def levels(key, dims, split, smallest, high):
    def one(dim, shards_of):
        heights = jax.random.uniform(jax.random.fold_in(jax.random.fold_in(key, 6), dim), (shards_of,), jnp.float32, smallest / len(split), high / len(split))
        return jnp.repeat(jnp.exp(heights), dims[dim] // shards_of).reshape((-1,) + (1,) * (len(dims) - dim - 1))

    gain = one(*split[0])
    for cut in split[1:]:
        gain = gain * one(*cut)
    return gain


def length_profile(amount, total, most, skew):
    weights = [(1 << 20) // math.isqrt(rank ** skew) + 1 for rank in range(2, amount + 1)]
    rest, counts = total - most - (amount - 1), [1] * (amount - 1)
    while rest > 0:
        candidates = [i for i in range(amount - 1) if counts[i] < most]
        pool, budget = sum([weights[i] for i in candidates]), rest
        for i in candidates:
            addition = min(most - counts[i], max(1, budget * weights[i] // pool), rest)
            counts[i] = counts[i] + addition
            rest = rest - addition
    return np.array([most] + counts)


def uneven(key, count, total, most, skew):
    if count == 2:
        one = jax.random.randint(key, (), max(1, total - most), min(most, total - 1) + 1)
        return jnp.stack([one, total - one])
    tallies = jnp.asarray(length_profile(count, total, most, skew), jnp.int32)
    pairs = (count - 1) // 2
    source_of, receiver = tallies[1:1 + 2 * pairs:2], tallies[2:2 + 2 * pairs:2]
    margin = jnp.minimum(source_of - 1, most - receiver)
    passed = jax.random.randint(jax.random.fold_in(key, 1), (pairs,), 0, 1 << 20) % (margin + 1)
    tallies = tallies.at[1:1 + 2 * pairs:2].set(source_of - passed).at[2:2 + 2 * pairs:2].set(receiver + passed)
    return tallies[jax.random.permutation(jax.random.fold_in(key, 2), count)]


def gaussian(key, dims, deviation, limit, shards=(), held_as=jnp.bfloat16):
    array = deviation * jax.random.normal(key, dims, jnp.float32)
    if shards:
        array = array * levels(key, dims, shards, -0.22, 0.18)
    return jnp.clip(array, -limit, limit).astype(held_as)


def setup_inputs(seed: int = 0) -> dict:
    splits = jax.random.split(jax.random.key(seed), 7)
    increment = gaussian(splits[0], (SLABS, NY, NX), 1.0, 6.0, ((1, 8), (2, 4)), jnp.float32)
    vert_rate = jnp.clip(jnp.exp(jax.random.uniform(splits[1], (VAR, LEV), jnp.float32, math.log(0.05), math.log(0.8))), 0.05, 0.8)
    zonal_rate = draw_zonal_rate(jax.random.fold_in(splits[6], 71), 0)
    merid_rate = jnp.clip(jnp.exp(jax.random.uniform(splits[3], (NBANDS, SLABS), jnp.float32, math.log(0.02), math.log(0.12))), 0.02, 0.12)
    lat_band = jnp.searchsorted(jnp.cumsum(uneven(splits[4], NBANDS, NY, 2 * NY // NBANDS, 0)), jnp.arange(NY), side="right").astype(jnp.int32)
    slab_owner = draw_slab_owner(jax.random.fold_in(splits[6], 71), 0)
    return dict(increment=increment, vert_rate=vert_rate, zonal_rate=zonal_rate, merid_rate=merid_rate, lat_band=lat_band, slab_owner=slab_owner)


def recursive_pass(values, decay, gains, reverse):
    zeros = jnp.zeros(values.shape[1:], values.dtype)
    if decay.ndim == values.ndim:

        def step(state, inputs):
            piece, dec, gain_now = inputs
            state = dec * state + gain_now * piece
            return (state, state)
        last_state, result = lax.scan(step, zeros, (values, decay, gains), reverse=reverse)
    else:

        def step_const(state, piece):
            state = decay * state + gains * piece
            return (state, state)
        last_state, result = lax.scan(step_const, zeros, values, reverse=reverse)
    return result

def smooth(values, rates):
    decay = 1.0 - rates
    gains = jnp.sqrt(rates * (2.0 - rates))
    forward = recursive_pass(values, decay, gains, False)
    return recursive_pass(forward, decay, gains, True)

def vertical_filter(values, vert_rate):
    stacked = values.reshape(VAR, LEV, NY, NX).transpose(1, 0, 2, 3)
    rates = vert_rate.T[:, :, None, None]
    result = smooth(stacked, rates)
    return result.transpose(1, 0, 2, 3).reshape(SLABS, NY, NX)

def reference(increment, vert_rate, zonal_rate, merid_rate, lat_band, slab_owner):
    vertical = vertical_filter(increment, vert_rate)
    zonal_rows = zonal_rate[lat_band].T
    zonal = smooth(vertical.transpose(2, 0, 1), zonal_rows).transpose(1, 2, 0)
    merid_rows = merid_rate[lat_band][:, :, None]
    smoothed = smooth(zonal.transpose(1, 0, 2), merid_rows).transpose(1, 0, 2)
    same = slab_owner[:, None] == slab_owner[None, :]
    earlier = jnp.arange(SLABS)[None, :] < jnp.arange(SLABS)[:, None]
    slot = lax.optimization_barrier(jnp.sum(jnp.logical_and(same, earlier), axis=1)).astype(jnp.int32)
    target = (slab_owner * CAP + slot).astype(jnp.int32)
    filtered_slabs = jnp.zeros((N_TX * CAP, NY, NX), smoothed.dtype).at[target].set(smoothed)
    covariance_product = vertical_filter(smoothed, vert_rate)
    return (covariance_product, filtered_slabs)
```

```python
import functools

import jax
import jax.numpy as jnp
from jax import lax
from jax.experimental import pallas as pl
from jax.experimental.pallas import tpu as pltpu
from jax.sharding import PartitionSpec as P

LEV = 16
VAR = 2
NBANDS = 16
CORES = 2
GROUP = 8
HIGHEST = lax.Precision.HIGHEST
VMEM_LIMIT = 48 * 1024 * 1024
SMEM = pl.BlockSpec(memory_space=pltpu.SMEM)
ANY = pl.BlockSpec(memory_space=pl.ANY)


def call(kernel, name, **how):
    return pl.pallas_call(
        kernel,
        compiler_params=pltpu.CompilerParams(vmem_limit_bytes=VMEM_LIMIT),
        cost_estimate=pl.CostEstimate(flops=0, bytes_accessed=4096, transcendentals=0),
        name=name,
        **how,
    )


def f32(*shape):
    return jax.ShapeDtypeStruct(shape, jnp.float32)


def i32(*shape):
    return jax.ShapeDtypeStruct(shape, jnp.int32)


def gain_of(rates):
    return jnp.sqrt(rates * (2.0 - rates))


def halves(x):
    high = x.astype(jnp.bfloat16)
    low = (x - high.astype(jnp.float32)).astype(jnp.bfloat16)
    return high, low


def exact_dot(a, b):
    return jnp.dot(a, b, precision=HIGHEST, preferred_element_type=jnp.float32)


def iota(shape, dim):
    return lax.broadcasted_iota(jnp.int32, shape, dim)


def select(table, band, shape):
    out = jnp.zeros(shape, jnp.float32)
    for b in range(NBANDS):
        entry = table[b : b + 1, :] if band.shape[1] == 1 else table[:, b : b + 1]
        out = jnp.where(band == b, entry, out)
    return out


def filter_levels(decay, gain, src_ref, dst_ref, rows, cut):
    state, held = None, []
    for level in range(LEV):
        piece = gain[level] * src_ref[level, rows, cut]
        state = piece if state is None else decay[level] * state + piece
        held.append(state)
    state = None
    for level in reversed(range(LEV)):
        piece = gain[level] * held[level]
        state = piece if state is None else decay[level] * state + piece
        dst_ref[level, rows, cut] = state


def level_factors(rate_ref):
    rates = [rate_ref[pl.program_id(0), level] for level in range(LEV)]
    decay = [1.0 - rate for rate in rates]
    gain = [jnp.sqrt(jnp.full((8, 128), rate * (2.0 - rate), jnp.float32))[:1, :1] for rate in rates]
    return decay, gain


def column_cuts(columns):
    width = 384 if columns % 384 == 0 else 128
    return [slice(start, start + width) for start in range(0, columns, width)]


def write_lists(chips, capacity, ladder, owner_ref, send_ref, recv_ref, slot_ref, held_ref, rank_ref, place_ref, step_ref, counts):
    slabs = owner_ref.shape[0]
    me = lax.axis_index("tx")
    chip = lax.div(me, CORES)
    for c in range(chips * (1 + CORES)):
        counts[c] = 0

    def clear(e, _):
        for d in range(chips - 1):
            send_ref[2 * capacity * d + e] = 0
        recv_ref[e] = 0
        slot_ref[e] = -1

        @pl.when(e < capacity)
        def _():
            held_ref[e] = -1

        return 0

    lax.fori_loop(0, 2 * capacity, clear, 0)

    def one(s, _):
        owner = owner_ref[s]
        its_chip = lax.div(owner, CORES)
        rank = counts[its_chip]
        slot = counts[chips + owner]
        counts[its_chip] = rank + 1
        counts[chips + owner] = slot + 1
        rank_ref[s] = rank
        place_ref[s] = slot
        for d in range(1, chips):

            @pl.when(its_chip == lax.rem(chip + d, chips))
            def _():
                send_ref[2 * capacity * (d - 1) + rank] = s

        @pl.when(its_chip == chip)
        def _():
            recv_ref[rank] = s
            slot_ref[rank] = jnp.where(owner == me, slot, -1)

            @pl.when(owner == me)
            def _():
                held_ref[slot] = slot

        return 0

    lax.fori_loop(0, slabs, one, 0)
    most = counts[0]
    for c in range(1, chips):
        most = jnp.maximum(most, counts[c])
    step = jnp.int32(0)
    for amount in ladder[:-1]:
        step = step + jnp.where(most > amount, 1, 0)
    step_ref[0] = step


def vertical_ends_kernel(chips, capacity, early, ladder, rate_ref, owner_ref, band_ref, zonal_ref, x_ref, *rest):
    v_ref, ends_ref = rest[:2]
    lists = rest[2:9]
    early_refs = rest[9 : 9 + chips - 1]
    counts, la_ref, sem = rest[9 + chips - 1 :]
    levels, rows, columns = x_ref.shape
    var = pl.program_id(0)

    @pl.when(var == 0)
    def _():
        write_lists(chips, capacity, ladder, owner_ref, *lists, counts)
        first = lax.axis_index("ty") * rows

        def fetch(r, _):
            la_ref[pl.ds(r, 1), :] = zonal_ref[pl.ds(band_ref[first + r], 1), :]
            return 0

        lax.fori_loop(0, rows, fetch, 0)
        la_ref[...] = jnp.log1p(-la_ref[...])
        ends_ref[...] = jnp.zeros(ends_ref.shape, jnp.float32)

    decay, gain = level_factors(rate_ref)
    lane = iota((1, 128), 1).astype(jnp.float32)
    slabs = la_ref.shape[1]
    slab_lane = iota((8, slabs), 1)
    blocks = columns // 128

    def eight(i, _):
        now = pl.ds(pl.multiple_of(i * 8, 8), 8)
        for cut in column_cuts(columns):
            filter_levels(decay, gain, x_ref, v_ref, now, cut)
        la_rows = la_ref[now, :]
        right_ends, left_ends = ends_ref[0, now, :], ends_ref[1, now, :]
        for level in range(levels):
            la = jnp.where(var == 1, la_rows[:, LEV + level : LEV + level + 1], la_rows[:, level : level + 1])
            la = jnp.broadcast_to(la, (8, 128))
            whole = jnp.exp(la * 128.0)
            pieces = [v_ref[level, now, b * 128 : (b + 1) * 128] for b in range(blocks)]
            right, left = pieces[0], pieces[-1]
            for b in range(1, blocks):
                right = whole * right + pieces[b]
                left = whole * left + pieces[blocks - 1 - b]
            right = jnp.sum(right * jnp.exp(la * (127.0 - lane)), axis=1, keepdims=True)
            left = jnp.sum(left * jnp.exp(la * lane), axis=1, keepdims=True)
            here = slab_lane == var * LEV + level
            right_ends = jnp.where(here, right, right_ends)
            left_ends = jnp.where(here, left, left_ends)
        ends_ref[0, now, :] = right_ends
        ends_ref[1, now, :] = left_ends
        return 0

    lax.fori_loop(0, rows // 8, eight, 0)
    send_ref = lists[0]
    for wait in (False, True):
        for d, early_ref in enumerate(early_refs):
            for e in range(early):
                slab = send_ref[2 * capacity * d + e]

                @pl.when(lax.div(slab, LEV) == var)
                def _():
                    copy = pltpu.make_async_copy(v_ref.at[lax.rem(slab, LEV)], early_ref.at[e], sem.at[d, e])
                    copy.wait() if wait else copy.start()


def vertical_ends(increment, vert_rate, zonal_rate, lat_band, slab_owner, chips, capacity, early, ladder):
    slabs, rows, columns = increment.shape
    spec = pl.BlockSpec((LEV, rows, columns), lambda v: (v, 0, 0))
    lists = [(chips - 1) * 2 * capacity, 2 * capacity, 2 * capacity, capacity, slabs, slabs, 1]
    outs = call(
        functools.partial(vertical_ends_kernel, chips, capacity, early, ladder),
        "vertical_ends",
        grid=(VAR,),
        in_specs=[SMEM, SMEM, SMEM, pl.BlockSpec(zonal_rate.shape, lambda v: (0, 0)), spec],
        out_specs=[spec, pl.BlockSpec((2, rows, slabs), lambda v: (0, 0, 0))] + [SMEM] * 7 + [ANY] * (chips - 1),
        out_shape=[f32(*increment.shape), f32(2, rows, slabs)]
        + [i32(n) for n in lists]
        + [f32(early, rows, columns)] * (chips - 1),
        scratch_shapes=[
            pltpu.SMEM((chips * (1 + CORES),), jnp.int32),
            pltpu.VMEM((rows, slabs), jnp.float32),
            pltpu.SemaphoreType.DMA((chips - 1, early)),
        ],
    )(vert_rate, slab_owner, lat_band, zonal_rate, increment)
    return outs[0], outs[1], outs[2:9], outs[9:]


def gate_kernel(*refs):
    pass


def gate(value, *after):
    return call(
        gate_kernel,
        "gate",
        in_specs=[ANY] * (1 + len(after)),
        out_specs=ANY,
        out_shape=jax.ShapeDtypeStruct(value.shape, value.dtype),
        input_output_aliases={0: 0},
    )(value, *after)


COLUMNS = 8


def tables_kernel(chips, devices, early, width, recv_ref, zonal_ref, merid_ref, merid_t_ref, band_ref, own_band_ref, row_ref, *rest):
    own_ends, twin_ends = rest[:chips], rest[chips : 2 * chips]
    t_ref, te_ref, r_ref, re_ref, coef_ref, coef_e_ref, hold = rest[2 * chips :]
    rows, slabs = own_ends[0].shape[1:]
    groups = chips * CORES
    me, place_y = lax.axis_index("tx"), lax.axis_index("ty")

    k, m = iota((rows, rows), 0), iota((rows, rows), 1)
    below, above = (k >= m).astype(jnp.float32), (k <= m).astype(jnp.float32)
    own_band = own_band_ref[...]
    la = jnp.log1p(-select(zonal_ref[...], own_band, (rows, slabs)))

    def tables_of(rates):
        log_decay = jnp.log1p(-rates)
        inclusive = exact_dot(below, log_decay)
        exclusive = inclusive - log_decay
        gains = gain_of(rates)
        sums = exact_dot(above, gains * jnp.exp(inclusive + exclusive))
        return inclusive, exclusive, gains, sums

    inclusive, exclusive, gains, sums = tables_of(select(merid_ref[...], own_band, (rows, slabs)))
    whole = jnp.exp(inclusive[rows - 1 :, :])
    before = gains * jnp.exp(-inclusive)
    after = jnp.exp(-exclusive)
    meridional = [whole * before, before * sums, after * sums, after, whole * after]

    tile_decay = jnp.exp(la * float(width))
    my_chip, my_core = lax.div(me, CORES), lax.rem(me, CORES)

    def ends_of(t, side):
        away = lax.rem(my_chip + chips - t // CORES, chips)
        out = jnp.zeros((rows, slabs), jnp.float32)
        for d in range(chips):
            value = jnp.where(my_core == t % CORES, own_ends[d][side], twin_ends[d][side])
            out = jnp.where(away == d, value, out)
        return out

    from_left = [jnp.zeros((rows, slabs), jnp.float32)]
    for t in range(groups):
        from_left.append(ends_of(t, 0) + tile_decay * from_left[-1])
    from_right = [-jnp.exp(la) * from_left[-1]]
    for t in reversed(range(1, groups)):
        from_right.append(ends_of(t, 1) + tile_decay * from_right[-1])
    from_right = from_right[::-1]

    def entering(tile):
        left = right = jnp.zeros((rows, slabs), jnp.float32)
        for t in range(groups):
            left = jnp.where(tile == t, from_left[t], left)
            right = jnp.where(tile == t, from_right[t], right)
        return left, right

    for c, table in enumerate([la, *entering(me), *meridional]):
        for g in range(slabs // GROUP):
            t_ref[g, c] = table[:, g * GROUP : (g + 1) * GROUP]
    slab, entry = iota((slabs, early), 0), iota((slabs, early), 1)
    hit = jnp.zeros((slabs, early), jnp.float32)
    for e in range(early):
        hit = jnp.where(jnp.logical_and(entry == e, slab == recv_ref[e]), 1.0, hit)
    common = [exact_dot(table, hit) for table in [la, *meridional]]
    for d in range(1, chips):
        left, right = entering(lax.rem(me + groups - CORES * d, groups))
        for c, table in enumerate([common[0], exact_dot(left, hit), exact_dot(right, hit), *common[1:]]):
            te_ref[d - 1, c] = table

    wide = 3 * rows
    k, m = iota((rows, wide), 0), iota((rows, wide), 1)
    m = m - jnp.where(m >= 2 * rows, 2 * rows, jnp.where(m >= rows, rows, 0))
    upto, onward = (k <= m).astype(jnp.float32), (k >= m).astype(jnp.float32)
    band_row = row_ref[...]
    rates = select(merid_t_ref[...], band_row, (slabs, wide))
    log_row = jnp.log1p(-rates[:, :rows])
    inclusive_row = exact_dot(log_row, upto)
    here = inclusive_row[:, :rows]
    sums_row = exact_dot(gain_of(rates[:, :rows]) * jnp.exp(2.0 * here - log_row), onward)
    before_row = gain_of(rates) * jnp.exp(-inclusive_row)
    after_row = before_row * sums_row
    for s in range(slabs):
        r_ref[s, 0:1] = before_row[s : s + 1]
        r_ref[s, 1:2] = after_row[s : s + 1]
    for e in range(early):
        re_ref[e] = r_ref[recv_ref[e]]

    decay, cross = [], []
    for n in range(devices):
        band = band_ref[n * rows : (n + 1) * rows]
        inclusive, _, _, sums = tables_of(select(merid_ref[...], band, (rows, slabs)))
        decay.append(jnp.exp(inclusive[rows - 1 :, :]))
        cross.append(sums[0:1, :])
    decay, cross = jnp.concatenate(decay, axis=0), jnp.concatenate(cross, axis=0)
    device = iota((devices, slabs), 0)
    own_f, own_bf, own_b = jnp.ones_like(decay), jnp.zeros_like(decay), jnp.ones_like(decay)
    stage, bit = 0, 1
    while bit < devices:
        upper = lax.rem(lax.div(device, bit), 2) == 1
        swap = lambda a: jnp.concatenate([a[n ^ bit : (n ^ bit) + 1] for n in range(devices)], axis=0)
        other_decay, other_cross = swap(decay), swap(cross)
        d_low, d_high = jnp.where(upper, other_decay, decay), jnp.where(upper, decay, other_decay)
        c_low, c_high = jnp.where(upper, other_cross, cross), jnp.where(upper, cross, other_cross)
        for c, table in enumerate([d_low, d_high, c_high, own_f, own_bf, own_b]):
            hold[...] = table
            coef_ref[stage, c : c + 1] = hold[pl.ds(place_y, 1), :]
        own_bf = jnp.where(upper, own_bf * d_low, own_bf + own_b * c_high * d_low)
        own_f = jnp.where(upper, own_f * d_low, own_f)
        own_b = jnp.where(upper, own_b, own_b * d_high)
        decay, cross = d_low * d_high, c_low + d_low * d_low * c_high
        coef_e_ref[stage] = exact_dot(coef_ref[stage], hit)
        stage, bit = stage + 1, 2 * bit


def tables(zonal_rate, merid_rate, lat_band, recv_slab, own_ends, twin_ends, columns, early):
    chips = len(own_ends)
    devices = lax.axis_size("ty")
    _, rows, slabs = own_ends[0].shape
    stages = (devices - 1).bit_length()
    own = lax.dynamic_slice_in_dim(lat_band, lax.axis_index("ty") * rows, rows)
    vmem = pl.BlockSpec(memory_space=pltpu.VMEM)
    return call(
        functools.partial(tables_kernel, chips, devices, early, columns),
        "tables",
        in_specs=[SMEM] + [vmem] * (6 + 2 * chips),
        out_specs=[vmem] * 6,
        out_shape=[
            f32(slabs // GROUP, COLUMNS, rows, GROUP),
            f32(chips - 1, COLUMNS, rows, early),
            f32(slabs, 2, 3 * rows),
            f32(early, 2, 3 * rows),
            f32(stages, 6, slabs),
            f32(stages, 6, early),
        ],
        scratch_shapes=[pltpu.VMEM((devices, slabs), jnp.float32)],
    )(
        recv_slab,
        zonal_rate,
        merid_rate,
        merid_rate.T,
        lat_band[:, None],
        own[:, None],
        jnp.tile(own, 3)[None, :],
        *own_ends,
        *twin_ends,
    )


def zonal_tile(v, la, left, right):
    rows, columns = v.shape
    block = 256 if columns % 256 == 0 else 128
    half = block // 2
    blocks = columns // block
    j, i = iota((block, block), 0), iota((block, block), 1)
    upto = jnp.where(j <= i, 1.0, 0.0).astype(jnp.bfloat16)
    onward = jnp.where(j >= i, 1.0, 0.0).astype(jnp.bfloat16)
    power = la * (iota((1, block), 1) - half).astype(jnp.float32)
    up, down = jnp.exp(power), jnp.exp(-power)
    value = [v[:, b * block : (b + 1) * block] for b in range(blocks)]

    def totals(scale, ones):
        parts = [halves(x * scale) for x in value]
        high = jnp.concatenate([p[0] for p in parts], axis=0)
        low = jnp.concatenate([p[1] for p in parts], axis=0)
        dot = functools.partial(jnp.dot, preferred_element_type=jnp.float32)
        total = dot(high, ones) + dot(low, ones)
        return [total[b * rows : (b + 1) * rows] for b in range(blocks)]

    enter = jnp.exp(la * (half + 1.0))
    state, rising = left, []
    for total in totals(down, upto):
        now = up * (total + enter * state)
        state = now[:, block - 1 :]
        rising.append(now)
    enter = jnp.exp(la * float(half))
    state, result = right, [None] * blocks
    parts = totals(up, onward)
    for b in reversed(range(blocks)):
        now = down * (parts[b] + enter * state)
        state = now[:, :1]
        result[b] = rising[b] + now - value[b]
    return result


def zonal_kernel(v_ref, t_ref, z_ref, o_ref):
    for s in range(v_ref.shape[0]):
        column = lambda c: t_ref[0, c, :, s : s + 1]
        result = zonal_tile(v_ref[s], column(0), column(1), column(2))
        block = result[0].shape[-1]
        for b, z in enumerate(result):
            cut = slice(b * block, (b + 1) * block)
            z_ref[s, :, cut] = z
            o_ref[0, s : s + 1, cut] = jnp.sum(z * column(3), axis=0, keepdims=True)
            o_ref[1, s : s + 1, cut] = jnp.sum(z * column(4), axis=0, keepdims=True)


def zonal(v, table):
    slabs, rows, columns = v.shape
    group = table.shape[-1]
    return call(
        zonal_kernel,
        "zonal",
        grid=(slabs // group,),
        in_specs=[
            pl.BlockSpec((group, rows, columns), lambda s: (s, 0, 0)),
            pl.BlockSpec((1, COLUMNS, rows, group), lambda s: (s, 0, 0, 0)),
        ],
        out_specs=[
            pl.BlockSpec((group, rows, columns), lambda s: (s, 0, 0)),
            pl.BlockSpec((2, group, columns), lambda s: (0, s, 0)),
        ],
        out_shape=[f32(*v.shape), f32(2, slabs, columns)],
    )(v, table)


def finish_tile(z, column, row_factors, f_in, b_in):
    rows = z.shape[0]
    wide = 3 * rows
    i, r = iota((rows, wide), 0), iota((rows, wide), 1)
    third = r >= 2 * rows
    r = r - jnp.where(third, 2 * rows, jnp.where(r >= rows, rows, 0))
    a, c = column(5), column(6)
    matrix = jnp.where(i >= r, a * row_factors[0:1], c * row_factors[1:2])
    high = matrix.astype(jnp.bfloat16)
    low = (matrix - high.astype(jnp.float32)).astype(jnp.bfloat16)
    matrix = jnp.where(third, low.astype(jnp.float32), high.astype(jnp.float32)).astype(jnp.bfloat16)
    z_high, z_low = halves(z)
    dot = functools.partial(jnp.dot, preferred_element_type=jnp.float32)
    if rows % 16 == 0:
        result = dot(matrix, jnp.concatenate([z_high, z_low, z_high], axis=0))
    else:
        result = dot(matrix[:, :rows], z_high) + dot(matrix[:, rows : 2 * rows], z_low)
        result = result + dot(matrix[:, 2 * rows :], z_high)
    return result + a * f_in + column(7) * b_in


def finish_kernel(chips, capacity, early, last, rate_ref, owner_ref, rank_ref, place_ref, held_ref, z_ref, t_ref, r_ref, s_ref, *rest):
    cov_ref = rest[0]
    late_refs, final_refs = rest[1:chips], rest[chips : 2 * chips - 1]
    twin_ref, out_ref, smooth, blank, sem, wipe_sem = rest[2 * chips - 1 :]
    levels, rows, columns = z_ref.shape
    var = pl.program_id(0)
    me = lax.axis_index("tx")
    my_chip = lax.div(me, CORES)
    first = pl.multiple_of(me * columns, 128)

    def wipe(wait):
        for e in range(capacity):

            @pl.when(jnp.logical_and(var == 0, held_ref[e] < 0))
            def _():
                copy = pltpu.make_async_copy(blank, out_ref.at[e], wipe_sem.at[e])
                copy.wait() if wait else copy.start()

    @pl.when(var == 0)
    def _():
        blank[...] = jnp.zeros(blank.shape, jnp.float32)

    wipe(False)

    def deliver(level, wait):
        slab = var * LEV + level
        owner, rank, slot = owner_ref[slab], rank_ref[slab], place_ref[slab]
        away = lax.rem(lax.div(owner, CORES) + chips - my_chip, chips)

        def move(condition, to):
            @pl.when(condition)
            def _():
                copy = pltpu.make_async_copy(smooth.at[level], to(), sem.at[level])
                copy.wait() if wait else copy.start()

        for d in range(1, chips):
            there = away == d
            middle = jnp.logical_and(rank >= early, rank < last)
            move(jnp.logical_and(there, middle), lambda: late_refs[d - 1].at[rank - early])
            move(jnp.logical_and(there, rank >= last), lambda: final_refs[d - 1].at[rank - last])
        move(owner == me, lambda: out_ref.at[slot, :, pl.ds(first, columns)])
        move(jnp.logical_and(away == 0, owner != me), lambda: twin_ref.at[slot])

    for level in range(levels):
        column = lambda c: t_ref[level // GROUP, c, :, level % GROUP : level % GROUP + 1]
        states = s_ref[:, level, :]
        smooth[level] = finish_tile(z_ref[level], column, r_ref[level], states[0:1], states[1:2])
        deliver(level, False)
    decay, gain = level_factors(rate_ref)

    def eight(i, _):
        now = pl.ds(pl.multiple_of(i * 8, 8), 8)
        for cut in column_cuts(columns):
            filter_levels(decay, gain, smooth, cov_ref, now, cut)
        return 0

    lax.fori_loop(0, rows // 8, eight, 0)
    for level in range(levels):
        deliver(level, True)
    wipe(True)


def finish(z, vert_rate, owner, rank, place_of, held, table, row_factors, states, chips, capacity, early, last, amount):
    slabs, rows, columns = z.shape
    outs = call(
        functools.partial(finish_kernel, chips, capacity, early, last),
        "finish",
        grid=(VAR,),
        in_specs=[SMEM] * 5
        + [
            pl.BlockSpec((LEV, rows, columns), lambda v: (v, 0, 0)),
            pl.BlockSpec((LEV // GROUP, COLUMNS, rows, GROUP), lambda v: (v, 0, 0, 0)),
            pl.BlockSpec((LEV, 2, 3 * rows), lambda v: (v, 0, 0)),
            pl.BlockSpec((2, LEV, columns), lambda v: (0, v, 0)),
        ],
        out_specs=[pl.BlockSpec((LEV, rows, columns), lambda v: (v, 0, 0))] + [ANY] * (2 * chips),
        out_shape=[f32(*z.shape)]
        + [f32(last - early, rows, columns)] * (chips - 1)
        + [f32(amount - last, rows, columns)] * (chips - 1)
        + [f32(capacity, rows, columns), f32(capacity, rows, chips * CORES * columns)],
        scratch_shapes=[
            pltpu.VMEM((LEV, rows, columns), jnp.float32),
            pltpu.VMEM((rows, chips * CORES * columns), jnp.float32),
            pltpu.SemaphoreType.DMA((LEV,)),
            pltpu.SemaphoreType.DMA((capacity,)),
        ],
    )(vert_rate, owner, rank, place_of, held, z, table, row_factors, states)
    return outs[0], outs[1:chips], outs[chips : 2 * chips - 1], outs[-2], outs[-1]


def finish_early_kernel(slot_ref, tile_ref, z_ref, t_ref, r_ref, s_ref, old_ref, done_ref, out_ref, sem):
    count, rows, columns = z_ref.shape
    first = pl.multiple_of(tile_ref[0] * columns, 128)
    for wait in (False, True):
        for e in range(count):
            if not wait:
                column = lambda c: t_ref[0, c, :, e : e + 1]
                states = s_ref[:, e, :]
                done_ref[e] = finish_tile(z_ref[e], column, r_ref[e], states[0:1], states[1:2])

            @pl.when(slot_ref[e] >= 0)
            def _():
                to = out_ref.at[slot_ref[e], :, pl.ds(first, columns)]
                copy = pltpu.make_async_copy(done_ref.at[e], to, sem.at[e])
                copy.wait() if wait else copy.start()


def finish_early(out, z, slot, tile, table, row_factors, states):
    count = z.shape[0]
    vmem = pl.BlockSpec(memory_space=pltpu.VMEM)
    return call(
        finish_early_kernel,
        "finish_early",
        in_specs=[SMEM, SMEM] + [vmem] * 4 + [ANY],
        out_specs=[vmem, ANY],
        out_shape=[f32(*z.shape), f32(*out.shape)],
        scratch_shapes=[pltpu.SemaphoreType.DMA((count,))],
        input_output_aliases={6: 1},
    )(slot, tile.reshape(1), z, table, row_factors, states, out)


def place_kernel(jobs, tile_ref, *rest):
    slots = rest[: len(jobs)]
    srcs = rest[len(jobs) : 2 * len(jobs)]
    out_ref, held, arrive, leave = rest[-4:]
    columns = held.shape[-1]
    entries, n = [], 0
    for k, (first, count) in enumerate(jobs):
        for e in range(count):
            entries.append((k, e, first + e, n))
            n += 1

    def read(k, e, at, n):
        return pltpu.make_async_copy(srcs[k].at[e], held.at[n], arrive.at[n])

    def write(k, e, at, n):
        start = pl.multiple_of(tile_ref[k] * columns, 128)
        return pltpu.make_async_copy(held.at[n], out_ref.at[slots[k][at], :, pl.ds(start, columns)], leave.at[n])

    def each(act):
        for k, e, at, n in entries:

            @pl.when(slots[k][at] >= 0)
            def _():
                act(k, e, at, n)

    def onward(*job):
        read(*job).wait()
        write(*job).start()

    each(lambda *job: read(*job).start())
    each(onward)
    each(lambda *job: write(*job).wait())


def place(out, jobs):
    n = sum(src.shape[0] for src, _, _, _ in jobs)
    count = len(jobs)
    return call(
        functools.partial(place_kernel, [(first, src.shape[0]) for src, _, first, _ in jobs]),
        "place",
        in_specs=[SMEM] * (1 + count) + [ANY] * (count + 1),
        out_specs=ANY,
        out_shape=f32(*out.shape),
        scratch_shapes=[
            pltpu.VMEM((n, *jobs[0][0].shape[1:]), jnp.float32),
            pltpu.SemaphoreType.DMA((n,)),
            pltpu.SemaphoreType.DMA((n,)),
        ],
        input_output_aliases={1 + 2 * count: 0},
    )(jnp.stack([job[3] for job in jobs]), *[job[1] for job in jobs], *[job[0] for job in jobs], out)


def scan_rows(states, coef):
    count = lax.axis_size("ty")
    place_y = lax.axis_index("ty")
    f_end, b_start = states[0], states[1]
    f_in = b_in = jnp.zeros_like(f_end)
    stage, bit = 0, 1
    while bit < count:
        upper = (place_y // bit) % 2 == 1
        pairs = [(i, i ^ bit) for i in range(count)]
        p_low, p_high, q_high, own_f, own_bf, own_b = [coef[stage, c][:, None] for c in range(6)]
        low = lambda mine, other: jnp.where(upper, other, mine)
        high = lambda mine, other: jnp.where(upper, mine, other)
        if 2 * bit < count:
            both = states if bit == 1 else jnp.stack([f_end, b_start])
            other_f, other_b = lax.ppermute(both, "ty", pairs)
            f_low, f_high = low(f_end, other_f), high(f_end, other_f)
            b_low, b_high = low(b_start, other_b), high(b_start, other_b)
        else:
            other = lax.ppermute(jnp.where(upper, b_start, f_end), "ty", pairs)
            f_low, b_high = low(f_end, other), high(b_start, other)
        from_above = b_high + q_high * f_low
        f_in = f_in + jnp.where(upper, own_f * f_low, 0.0)
        b_in = b_in + jnp.where(upper, own_bf * f_low, own_b * from_above)
        if 2 * bit < count:
            f_end = f_high + p_high * f_low
            b_start = b_low + p_low * from_above
        stage, bit = stage + 1, 2 * bit
    return jnp.stack([f_in, b_in])


def run(amount, early, vert_rate, zonal_rate, merid_rate, lat_band, slab_owner, v, ends, lists, early_sent):
    slabs, rows, columns = v.shape
    groups = lax.axis_size("tx")
    chips = groups // CORES
    capacity = 2 * slabs // groups
    me = lax.axis_index("tx")
    twin = me ^ 1
    last = max(amount - max(capacity // 8, 1), early + 1)
    twins = [(i, i ^ 1) for i in range(groups)]
    hop = lambda d: [(i, (i + CORES * d) % groups) for i in range(groups)]
    across = lambda values: [lax.ppermute(a, "tx", hop(d + 1)) for d, a in enumerate(values)]
    offsets = range(1, chips)
    source_of = lambda who, d: (who + groups - CORES * d) % groups
    _, recv_slab, recv_slot, held, rank, place_of, _ = lists

    own_ends = [ends, *across([ends] * (chips - 1))]
    early_v = across([gate(a, *own_ends[1:]) for a in early_sent])
    twin_ends = [lax.ppermute(a, "tx", twins) for a in own_ends]
    table, table_e, row_factors, row_factors_e, coef, coef_e = tables(
        zonal_rate, merid_rate, lat_band, recv_slab, own_ends, twin_ends, columns, early
    )
    z, states = zonal(v, table)
    covariance, late, final, twin_sent, out = finish(
        z,
        vert_rate,
        slab_owner,
        rank,
        place_of,
        held,
        table,
        row_factors,
        scan_rows(states, coef),
        chips,
        capacity,
        early,
        last,
        amount,
    )
    from_twin = lax.ppermute(twin_sent, "tx", twins)
    late, final = across(late), across(final)
    jobs = [(from_twin, held, 0, twin)]
    for d in offsets:
        early_z, states = zonal(gate(early_v[d - 1], out), table_e[d - 1 : d])
        entering = scan_rows(states, coef_e)
        done, out = finish_early(out, early_z, recv_slot, source_of(me, d), table_e[d - 1 : d], row_factors_e, entering)
        jobs.append((lax.ppermute(done, "tx", twins), recv_slot, 0, source_of(twin, d)))
    out = place(out, jobs)
    for first, arrived in ((early, late), (last, final)):
        arrived = [gate(a, out) for a in arrived] if first == early else arrived
        jobs = []
        for d in offsets:
            jobs.append((arrived[d - 1], recv_slot, first, source_of(me, d)))
            jobs.append((lax.ppermute(arrived[d - 1], "tx", twins), recv_slot, first, source_of(twin, d)))
        out = place(out, jobs)
    return covariance, out


def shards(increment, vert_rate, zonal_rate, merid_rate, lat_band, slab_owner):
    slabs = increment.shape[0]
    groups = lax.axis_size("tx")
    capacity = 2 * slabs // groups
    early = 3 * capacity // 4
    ladder = sorted({-(-capacity * n // 16) for n in (21, 22, 32)})
    v, ends, lists, early_sent = vertical_ends(
        increment, vert_rate, zonal_rate, lat_band, slab_owner, groups // CORES, capacity, early, ladder
    )
    return lax.switch(
        lists[-1][0],
        [functools.partial(run, amount, early) for amount in ladder],
        vert_rate,
        zonal_rate,
        merid_rate,
        lat_band,
        slab_owner,
        v,
        ends,
        lists,
        early_sent,
    )


def solution(mesh):
    return jax.shard_map(
        shards,
        mesh=mesh,
        in_specs=(P(None, "ty", "tx"), P(), P(), P(), P(), P()),
        out_specs=(P(None, "ty", "tx"), P("tx", "ty", None)),
        check_vma=False,
    )
```

```python
import functools

import jax
import jax.numpy as jnp
from jax import lax
from jax.experimental import pallas as pl
from jax.experimental.pallas import tpu as pltpu
from jax.sharding import PartitionSpec as P

LEV = 16
VAR = 2
NBANDS = 16
CORES = 2
GROUP = 8
HIGHEST = lax.Precision.HIGHEST
VMEM_LIMIT = 48 * 1024 * 1024
SMEM = pl.BlockSpec(memory_space=pltpu.SMEM)
ANY = pl.BlockSpec(memory_space=pl.ANY)


def call(kernel, name, **how):
    return pl.pallas_call(
        kernel,
        compiler_params=pltpu.CompilerParams(vmem_limit_bytes=VMEM_LIMIT),
        cost_estimate=pl.CostEstimate(flops=0, bytes_accessed=4096, transcendentals=0),
        name=name,
        **how,
    )


def f32(*shape):
    return jax.ShapeDtypeStruct(shape, jnp.float32)


def i32(*shape):
    return jax.ShapeDtypeStruct(shape, jnp.int32)


def gain_of(rates):
    return jnp.sqrt(rates * (2.0 - rates))


def halves(x):
    high = x.astype(jnp.bfloat16)
    low = (x - high.astype(jnp.float32)).astype(jnp.bfloat16)
    return high, low


def exact_dot(a, b):
    return jnp.dot(a, b, precision=HIGHEST, preferred_element_type=jnp.float32)


def iota(shape, dim):
    return lax.broadcasted_iota(jnp.int32, shape, dim)


def select(table, band, shape):
    out = jnp.zeros(shape, jnp.float32)
    for b in range(NBANDS):
        entry = table[b : b + 1, :] if band.shape[1] == 1 else table[:, b : b + 1]
        out = jnp.where(band == b, entry, out)
    return out


def filter_levels(decay, gain, src_ref, dst_ref, rows, cut):
    state, held = None, []
    for level in range(LEV):
        piece = gain[level] * src_ref[level, rows, cut]
        state = piece if state is None else decay[level] * state + piece
        held.append(state)
    state = None
    for level in reversed(range(LEV)):
        piece = gain[level] * held[level]
        state = piece if state is None else decay[level] * state + piece
        dst_ref[level, rows, cut] = state


def level_factors(rate_ref, var):
    rates = [rate_ref[var, level] for level in range(LEV)]
    decay = [1.0 - rate for rate in rates]
    gain = [jnp.sqrt(jnp.full((8, 128), rate * (2.0 - rate), jnp.float32))[:1, :1] for rate in rates]
    return decay, gain


def column_cuts(columns):
    width = 384 if columns % 384 == 0 else 128
    return [slice(start, start + width) for start in range(0, columns, width)]


def write_lists(chips, capacity, head, ladder, owner_ref, send_ref, recv_ref, slot_ref, held_ref, rank_ref, place_ref, step_ref, counts):
    slabs = owner_ref.shape[0]
    me = lax.axis_index("tx")
    chip = lax.div(me, CORES)
    for c in range(chips * (1 + CORES)):
        counts[c] = 0

    def clear(e, _):
        for d in range(chips - 1):
            send_ref[2 * capacity * d + e] = 0
        recv_ref[e] = 0
        slot_ref[e] = -1

        @pl.when(e < capacity)
        def _():
            held_ref[e] = -1

        return 0

    lax.fori_loop(0, 2 * capacity, clear, 0)

    def one(s, _):
        owner = owner_ref[s]
        its_chip = lax.div(owner, CORES)
        rank = counts[its_chip]
        slot = counts[chips + owner]
        counts[its_chip] = rank + 1
        counts[chips + owner] = slot + 1
        rank_ref[s] = rank
        place_ref[s] = slot
        for d in range(1, chips):

            @pl.when(its_chip == lax.rem(chip + d, chips))
            def _():
                send_ref[2 * capacity * (d - 1) + rank] = s

        @pl.when(its_chip == chip)
        def _():
            recv_ref[rank] = s
            slot_ref[rank] = jnp.where(owner == me, slot, -1)

            @pl.when(owner == me)
            def _():
                held_ref[slot] = slot

        return 0

    lax.fori_loop(0, LEV, one, 0)
    for c in range(chips):
        counts[c] = jnp.maximum(counts[c], head)
    lax.fori_loop(LEV, slabs, one, 0)
    most = counts[0]
    for c in range(1, chips):
        most = jnp.maximum(most, counts[c])
    step = jnp.int32(0)
    for amount in ladder[:-1]:
        step = step + jnp.where(most > amount, 1, 0)
    step_ref[0] = step


def vertical_kernel(var, chips, capacity, early, head, ladder, rate_ref, owner_ref, x_ref, *rest):
    if var == 0:
        lists, v_ref, first_refs, rest_refs = rest[:7], rest[7], rest[8 : 7 + chips], rest[7 + chips : 6 + 2 * chips]
        counts, sem = rest[-2:]
        send_ref = lists[0]

        @pl.when(pl.program_id(0) == 0)
        def _():
            write_lists(chips, capacity, head, ladder, owner_ref, *lists, counts)
    else:
        send_ref, v_ref, first_refs, rest_refs = rest[0], rest[1 + chips], (), rest[2 + chips : 1 + 2 * chips]
        sem = rest[-1]
    _, rows, columns = x_ref.shape
    step, steps = pl.program_id(0), pl.num_programs(0)
    decay, gain = level_factors(rate_ref, var)

    def eight(i, _):
        now = pl.ds(pl.multiple_of(i * 8, 8), 8)
        for cut in column_cuts(columns):
            filter_levels(decay, gain, x_ref, v_ref, now, cut)
        return 0

    lax.fori_loop(0, rows // 8, eight, 0)
    here = pl.ds(pl.multiple_of(step * rows, 8), rows)
    for d in range(chips - 1):
        for e in range(0 if var == 0 else head, early):
            slab = send_ref[2 * capacity * d + e]
            to_ref, at = (first_refs[d], e) if e < head else (rest_refs[d], e - head)

            @pl.when(lax.div(slab, LEV) == var)
            def _():
                from_ref = v_ref.at[lax.rem(slab, LEV)]
                pltpu.make_async_copy(from_ref, to_ref.at[at, here], sem.at[step, d, e]).start()

    @pl.when(step == steps - 1)
    def _():
        for d in range(chips - 1):
            for e in range(0 if var == 0 else head, early):
                slab = send_ref[2 * capacity * d + e]
                to_ref, at = (first_refs[d], e) if e < head else (rest_refs[d], e - head)

                @pl.when(lax.div(slab, LEV) == var)
                def _():
                    for n in range(steps):
                        pltpu.make_async_copy(v_ref.at[0], to_ref.at[at, here], sem.at[n, d, e]).wait()


def vertical_first(increment, vert_rate, slab_owner, chips, capacity, early, head, ladder):
    slabs, rows, columns = increment.shape
    steps = 2 if rows % 16 == 0 else 1
    spec = pl.BlockSpec((LEV, rows // steps, columns), lambda r: (0, r, 0))
    lists = [(chips - 1) * 2 * capacity, 2 * capacity, 2 * capacity, capacity, slabs, slabs, 1]
    outs = call(
        functools.partial(vertical_kernel, 0, chips, capacity, early, head, ladder),
        "vertical_first",
        grid=(steps,),
        in_specs=[SMEM, SMEM, spec],
        out_specs=[SMEM] * 7 + [spec] + [ANY] * (2 * chips - 2),
        out_shape=[i32(n) for n in lists]
        + [f32(*increment.shape)]
        + [f32(head, rows, columns)] * (chips - 1)
        + [f32(early - head, rows, columns)] * (chips - 1),
        scratch_shapes=[
            pltpu.SMEM((chips * (1 + CORES),), jnp.int32),
            pltpu.SemaphoreType.DMA((steps, chips - 1, early)),
        ],
    )(vert_rate, slab_owner, increment)
    return outs[:7], outs[7], outs[8 : 7 + chips], outs[7 + chips :]


def vertical_second(increment, vert_rate, slab_owner, send, v, rest_sent, early, head):
    slabs, rows, columns = increment.shape
    chips = 1 + len(rest_sent)
    capacity = send.shape[0] // (2 * (chips - 1))
    steps = 2 if rows % 16 == 0 else 1
    spec = pl.BlockSpec((LEV, rows // steps, columns), lambda r: (1, r, 0))
    outs = call(
        functools.partial(vertical_kernel, 1, chips, capacity, early, head, ()),
        "vertical_second",
        grid=(steps,),
        in_specs=[SMEM, SMEM, spec, SMEM] + [ANY] * chips,
        out_specs=[spec] + [ANY] * (chips - 1),
        out_shape=[f32(*v.shape)] + [f32(*a.shape) for a in rest_sent],
        scratch_shapes=[pltpu.SemaphoreType.DMA((steps, chips - 1, early))],
        input_output_aliases={4 + n: n for n in range(chips)},
    )(vert_rate, slab_owner, increment, send, v, *rest_sent)
    return outs[0], outs[1:]


def ends_kernel(band_ref, zonal_ref, v_ref, ends_ref, la_ref):
    levels, rows, columns = v_ref.shape
    var = pl.program_id(0)

    @pl.when(var == 0)
    def _():
        first = lax.axis_index("ty") * rows

        def fetch(r, _):
            la_ref[pl.ds(r, 1), :] = zonal_ref[pl.ds(band_ref[first + r], 1), :]
            return 0

        lax.fori_loop(0, rows, fetch, 0)
        la_ref[...] = jnp.log1p(-la_ref[...])
        ends_ref[...] = jnp.zeros(ends_ref.shape, jnp.float32)

    lane = iota((1, 128), 1).astype(jnp.float32)
    slabs = la_ref.shape[1]
    slab_lane = iota((8, slabs), 1)
    blocks = columns // 128

    def row_sums(parts):
        high, low = halves(jnp.concatenate(parts, axis=0))
        ones = jnp.ones((128, 128), jnp.bfloat16)
        dot = functools.partial(jnp.dot, preferred_element_type=jnp.float32)
        return dot(high, ones) + dot(low, ones)

    def eight(i, _):
        now = pl.ds(pl.multiple_of(i * 8, 8), 8)
        la_rows = jnp.where(var == 1, la_ref[now, LEV:], la_ref[now, :LEV])
        whole_rows = jnp.exp(la_rows * 128.0)
        rights, lefts = [], []
        for level in range(levels):
            la = jnp.broadcast_to(la_rows[:, level : level + 1], (8, 128))
            whole = jnp.broadcast_to(whole_rows[:, level : level + 1], (8, 128))
            pieces = [v_ref[level, now, b * 128 : (b + 1) * 128] for b in range(blocks)]
            right, left = pieces[0], pieces[-1]
            for b in range(1, blocks):
                right = whole * right + pieces[b]
                left = whole * left + pieces[blocks - 1 - b]
            rights.append(right * jnp.exp(la * (127.0 - lane)))
            lefts.append(left * jnp.exp(la * lane))
        right, left = row_sums(rights), row_sums(lefts)
        right_ends, left_ends = ends_ref[0, now, :], ends_ref[1, now, :]
        for level in range(levels):
            here = slab_lane == var * LEV + level
            right_ends = jnp.where(here, right[level * 8 : (level + 1) * 8, :slabs], right_ends)
            left_ends = jnp.where(here, left[level * 8 : (level + 1) * 8, :slabs], left_ends)
        ends_ref[0, now, :] = right_ends
        ends_ref[1, now, :] = left_ends
        return 0

    lax.fori_loop(0, rows // 8, eight, 0, unroll=2 if rows % 16 == 0 else 1)


def zonal_ends(v, zonal_rate, lat_band):
    slabs, rows, columns = v.shape
    return call(
        ends_kernel,
        "ends",
        grid=(VAR,),
        in_specs=[
            SMEM,
            pl.BlockSpec(zonal_rate.shape, lambda v: (0, 0)),
            pl.BlockSpec((LEV, rows, columns), lambda v: (v, 0, 0)),
        ],
        out_specs=pl.BlockSpec((2, rows, slabs), lambda v: (0, 0, 0)),
        out_shape=f32(2, rows, slabs),
        scratch_shapes=[pltpu.VMEM((rows, slabs), jnp.float32)],
    )(lat_band, zonal_rate, v)


def gate_kernel(*refs):
    pass


def gate(value, *after):
    return call(
        gate_kernel,
        "gate",
        in_specs=[ANY] * (1 + len(after)),
        out_specs=ANY,
        out_shape=jax.ShapeDtypeStruct(value.shape, value.dtype),
        input_output_aliases={0: 0},
    )(value, *after)


COLUMNS = 8


def tables_kernel(chips, devices, early, width, recv_ref, zonal_ref, merid_ref, merid_t_ref, band_ref, own_band_ref, row_ref, *rest):
    own_ends, twin_ends = rest[:chips], rest[chips : 2 * chips]
    t_ref, te_ref, r_ref, re_ref, coef_ref, hold = rest[2 * chips :]
    rows, slabs = own_ends[0].shape[1:]
    groups = chips * CORES
    me, place_y = lax.axis_index("tx"), lax.axis_index("ty")

    k, m = iota((rows, rows), 0), iota((rows, rows), 1)
    below, above = (k >= m).astype(jnp.float32), (k <= m).astype(jnp.float32)
    own_band = own_band_ref[...]
    la = jnp.log1p(-select(zonal_ref[...], own_band, (rows, slabs)))

    def tables_of(rates):
        log_decay = jnp.log1p(-rates)
        inclusive = exact_dot(below, log_decay)
        exclusive = inclusive - log_decay
        gains = gain_of(rates)
        sums = exact_dot(above, gains * jnp.exp(inclusive + exclusive))
        return inclusive, exclusive, gains, sums

    inclusive, exclusive, gains, sums = tables_of(select(merid_ref[...], own_band, (rows, slabs)))
    whole = jnp.exp(inclusive[rows - 1 :, :])
    before = gains * jnp.exp(-inclusive)
    after = jnp.exp(-exclusive)
    meridional = [whole * before, before * sums, after * sums, after, whole * after]

    tile_decay = jnp.exp(la * float(width))
    my_chip, my_core = lax.div(me, CORES), lax.rem(me, CORES)

    def ends_of(t, side):
        away = lax.rem(my_chip + chips - t // CORES, chips)
        out = jnp.zeros((rows, slabs), jnp.float32)
        for d in range(chips):
            value = jnp.where(my_core == t % CORES, own_ends[d][side], twin_ends[d][side])
            out = jnp.where(away == d, value, out)
        return out

    from_left = [jnp.zeros((rows, slabs), jnp.float32)]
    for t in range(groups):
        from_left.append(ends_of(t, 0) + tile_decay * from_left[-1])
    from_right = [-jnp.exp(la) * from_left[-1]]
    for t in reversed(range(1, groups)):
        from_right.append(ends_of(t, 1) + tile_decay * from_right[-1])
    from_right = from_right[::-1]

    def entering(tile):
        left = right = jnp.zeros((rows, slabs), jnp.float32)
        for t in range(groups):
            left = jnp.where(tile == t, from_left[t], left)
            right = jnp.where(tile == t, from_right[t], right)
        return left, right

    for c, table in enumerate([la, *entering(me), *meridional]):
        for g in range(slabs // GROUP):
            t_ref[g, c] = table[:, g * GROUP : (g + 1) * GROUP]
    slab, entry = iota((slabs, early), 0), iota((slabs, early), 1)
    hit = jnp.zeros((slabs, early), jnp.float32)
    for e in range(early):
        hit = jnp.where(jnp.logical_and(entry == e, slab == recv_ref[e]), 1.0, hit)
    common = [exact_dot(table, hit) for table in [la, *meridional]]
    for d in range(1, chips):
        left, right = entering(lax.rem(me + groups - CORES * d, groups))
        for c, table in enumerate([common[0], exact_dot(left, hit), exact_dot(right, hit), *common[1:]]):
            te_ref[d - 1, c] = table

    wide = 3 * rows
    k, m = iota((rows, wide), 0), iota((rows, wide), 1)
    m = m - jnp.where(m >= 2 * rows, 2 * rows, jnp.where(m >= rows, rows, 0))
    upto, onward = (k <= m).astype(jnp.float32), (k >= m).astype(jnp.float32)
    band_row = row_ref[...]
    rates = select(merid_t_ref[...], band_row, (slabs, wide))
    log_row = jnp.log1p(-rates[:, :rows])
    inclusive_row = exact_dot(log_row, upto)
    here = inclusive_row[:, :rows]
    sums_row = exact_dot(gain_of(rates[:, :rows]) * jnp.exp(2.0 * here - log_row), onward)
    before_row = gain_of(rates) * jnp.exp(-inclusive_row)
    after_row = before_row * sums_row
    for s in range(slabs):
        r_ref[s, 0:1] = before_row[s : s + 1]
        r_ref[s, 1:2] = after_row[s : s + 1]
    for e in range(early):
        re_ref[e] = r_ref[recv_ref[e]]

    decay, cross = [], []
    for n in range(devices):
        band = band_ref[n * rows : (n + 1) * rows]
        inclusive, _, _, sums = tables_of(select(merid_ref[...], band, (rows, slabs)))
        decay.append(jnp.exp(inclusive[rows - 1 :, :]))
        cross.append(sums[0:1, :])
    decay, cross = jnp.concatenate(decay, axis=0), jnp.concatenate(cross, axis=0)
    device = iota((devices, slabs), 0)
    own_f, own_bf, own_b = jnp.ones_like(decay), jnp.zeros_like(decay), jnp.ones_like(decay)
    stage, bit = 0, 1
    while bit < devices:
        upper = lax.rem(lax.div(device, bit), 2) == 1
        swap = lambda a: jnp.concatenate([a[n ^ bit : (n ^ bit) + 1] for n in range(devices)], axis=0)
        other_decay, other_cross = swap(decay), swap(cross)
        d_low, d_high = jnp.where(upper, other_decay, decay), jnp.where(upper, decay, other_decay)
        c_low, c_high = jnp.where(upper, other_cross, cross), jnp.where(upper, cross, other_cross)
        for c, table in enumerate([d_low, d_high, c_high, own_f, own_bf, own_b]):
            hold[...] = table
            coef_ref[stage, c : c + 1] = hold[pl.ds(place_y, 1), :]
        own_bf = jnp.where(upper, own_bf * d_low, own_bf + own_b * c_high * d_low)
        own_f = jnp.where(upper, own_f * d_low, own_f)
        own_b = jnp.where(upper, own_b, own_b * d_high)
        decay, cross = d_low * d_high, c_low + d_low * d_low * c_high
        stage, bit = stage + 1, 2 * bit


def tables(zonal_rate, merid_rate, lat_band, recv_slab, own_ends, twin_ends, columns, early):
    chips = len(own_ends)
    devices = lax.axis_size("ty")
    _, rows, slabs = own_ends[0].shape
    stages = (devices - 1).bit_length()
    own = lax.dynamic_slice_in_dim(lat_band, lax.axis_index("ty") * rows, rows)
    vmem = pl.BlockSpec(memory_space=pltpu.VMEM)
    return call(
        functools.partial(tables_kernel, chips, devices, early, columns),
        "tables",
        in_specs=[SMEM] + [vmem] * (6 + 2 * chips),
        out_specs=[vmem] * 5,
        out_shape=[
            f32(slabs // GROUP, COLUMNS, rows, GROUP),
            f32(chips - 1, COLUMNS, rows, early),
            f32(slabs, 2, 3 * rows),
            f32(early, 2, 3 * rows),
            f32(stages, 6, slabs),
        ],
        scratch_shapes=[pltpu.VMEM((devices, slabs), jnp.float32)],
    )(
        recv_slab,
        zonal_rate,
        merid_rate,
        merid_rate.T,
        lat_band[:, None],
        own[:, None],
        jnp.tile(own, 3)[None, :],
        *own_ends,
        *twin_ends,
    )


def zonal_tile(v, la, left, right, block):
    rows, columns = v.shape
    half = block // 2
    blocks = columns // block
    j, i = iota((block, block), 0), iota((block, block), 1)
    upto = jnp.where(j <= i, 1.0, 0.0).astype(jnp.bfloat16)
    onward = jnp.where(j >= i, 1.0, 0.0).astype(jnp.bfloat16)
    power = la * (iota((1, block), 1) - half).astype(jnp.float32)
    up, down = jnp.exp(power), jnp.exp(-power)
    value = [v[:, b * block : (b + 1) * block] for b in range(blocks)]

    def totals(scale, ones):
        parts = [halves(x * scale) for x in value]
        high = jnp.concatenate([p[0] for p in parts], axis=0)
        low = jnp.concatenate([p[1] for p in parts], axis=0)
        dot = functools.partial(jnp.dot, preferred_element_type=jnp.float32)
        total = dot(high, ones) + dot(low, ones)
        return [total[b * rows : (b + 1) * rows] for b in range(blocks)]

    enter = jnp.exp(la * (half + 1.0))
    state, rising = left, []
    for total in totals(down, upto):
        now = up * (total + enter * state)
        state = now[:, block - 1 :]
        rising.append(now)
    enter = jnp.exp(la * float(half))
    state, result = right, [None] * blocks
    parts = totals(up, onward)
    for b in reversed(range(blocks)):
        now = down * (parts[b] + enter * state)
        state = now[:, :1]
        result[b] = rising[b] + now - value[b]
    return result


def zonal_kernel(first, v_ref, t_ref, z_ref, o_ref):
    for s in range(v_ref.shape[0]):
        block = 256 if v_ref.shape[-1] % 256 == 0 else 128
        column = lambda c: jnp.broadcast_to(t_ref[0, c, :, first + s : first + s + 1], (t_ref.shape[2], block))
        result = zonal_tile(v_ref[s], column(0), column(1), column(2), block)
        for side in range(2):
            weight = column(3 + side)
            for b, z in enumerate(result):
                o_ref[side, s : s + 1, b * block : (b + 1) * block] = jnp.sum(z * weight, axis=0, keepdims=True)
        for b, z in enumerate(result):
            z_ref[s, :, b * block : (b + 1) * block] = z


def zonal(v, table, first=0):
    slabs, rows, columns = v.shape
    group = min(table.shape[-1], slabs)
    return call(
        functools.partial(zonal_kernel, first),
        "zonal",
        grid=(slabs // group,),
        in_specs=[
            pl.BlockSpec((group, rows, columns), lambda s: (s, 0, 0)),
            pl.BlockSpec((1, *table.shape[1:]), lambda s: (s, 0, 0, 0)),
        ],
        out_specs=[
            pl.BlockSpec((group, rows, columns), lambda s: (s, 0, 0)),
            pl.BlockSpec((2, group, columns), lambda s: (0, s, 0)),
        ],
        out_shape=[f32(*v.shape), f32(2, slabs, columns)],
    )(v, table)


def finish_tile(z, column, row_factors, f_in, b_in):
    rows = z.shape[0]
    wide = 3 * rows
    i, r = iota((rows, wide), 0), iota((rows, wide), 1)
    third = r >= 2 * rows
    r = r - jnp.where(third, 2 * rows, jnp.where(r >= rows, rows, 0))
    a, c = column(5), column(6)
    matrix = jnp.where(i >= r, a * row_factors[0:1], c * row_factors[1:2])
    high = matrix.astype(jnp.bfloat16)
    low = (matrix - high.astype(jnp.float32)).astype(jnp.bfloat16)
    matrix = jnp.where(third, low.astype(jnp.float32), high.astype(jnp.float32)).astype(jnp.bfloat16)
    z_high, z_low = halves(z)
    dot = functools.partial(jnp.dot, preferred_element_type=jnp.float32)
    if rows % 16 == 0:
        result = dot(matrix, jnp.concatenate([z_high, z_low, z_high], axis=0))
    else:
        result = dot(matrix[:, :rows], z_high) + dot(matrix[:, rows : 2 * rows], z_low)
        result = result + dot(matrix[:, 2 * rows :], z_high)
    return result + a * f_in + column(7) * b_in


def finish_kernel(chips, capacity, bounds, twin_bounds, rate_ref, owner_ref, rank_ref, place_ref, held_ref, z_ref, t_ref, r_ref, s_ref, *rest):
    cov_ref = rest[0]
    chunk_refs = [rest[1 + k * (chips - 1) : 1 + (k + 1) * (chips - 1)] for k in range(len(bounds))]
    rest = rest[1 + len(bounds) * (chips - 1) :]
    twin_refs, rest = rest[: len(twin_bounds)], rest[len(twin_bounds) :]
    out_ref, smooth, blank, early_states, sem, wipe_sem, state_sem = rest
    early = bounds[0][0]
    levels, rows, columns = z_ref.shape
    var = pl.program_id(0)
    me = lax.axis_index("tx")
    my_chip = lax.div(me, CORES)
    first = pl.multiple_of(me * columns, 128)

    def wipe(wait):
        for e in range(capacity):

            @pl.when(jnp.logical_and(var == 0, held_ref[e] < 0))
            def _():
                copy = pltpu.make_async_copy(blank, out_ref.at[e], wipe_sem.at[e])
                copy.wait() if wait else copy.start()

    @pl.when(var == 0)
    def _():
        blank[...] = jnp.zeros(blank.shape, jnp.float32)
        early_states[...] = jnp.zeros(early_states.shape, jnp.float32)

    wipe(False)

    def deliver(level, wait):
        slab = var * LEV + level
        owner, rank, slot = owner_ref[slab], rank_ref[slab], place_ref[slab]
        away = lax.rem(lax.div(owner, CORES) + chips - my_chip, chips)

        def move(condition, to):
            @pl.when(condition)
            def _():
                copy = pltpu.make_async_copy(smooth.at[level], to(), sem.at[level])
                copy.wait() if wait else copy.start()

        for d in range(1, chips):
            there = away == d
            for (a, b), refs in zip(bounds, chunk_refs):
                within = jnp.logical_and(there, jnp.logical_and(rank >= a, rank < b))
                at = pl.multiple_of((rank - a) * rows, 8)
                move(within, lambda: refs[d - 1].at[pl.ds(at, rows)])
            if not wait:

                @pl.when(jnp.logical_and(there, rank < early))
                def _():
                    early_states[d - 1, pl.ds(rank, 1), :] = s_ref[0, level : level + 1, :]
                    early_states[d - 1, pl.ds(early + rank, 1), :] = s_ref[1, level : level + 1, :]
        move(owner == me, lambda: out_ref.at[slot, :, pl.ds(first, columns)])
        for (a, b), ref in zip(twin_bounds, twin_refs):
            within = jnp.logical_and(slot >= a, slot < b)
            at = pl.multiple_of((slot - a) * rows, 8)
            move(jnp.logical_and(jnp.logical_and(away == 0, owner != me), within), lambda: ref.at[pl.ds(at, rows)])

    for level in range(levels):
        column = lambda c: t_ref[level // GROUP, c, :, level % GROUP : level % GROUP + 1]
        states = s_ref[:, level, :]
        smooth[level] = finish_tile(z_ref[level], column, r_ref[level], states[0:1], states[1:2])
        deliver(level, False)

    def send_states(wait):
        for d in range(1, chips):

            @pl.when(var == VAR - 1)
            def _():
                to = chunk_refs[0][d - 1].at[pl.ds((bounds[0][1] - early) * rows, early_states.shape[1])]
                copy = pltpu.make_async_copy(early_states.at[d - 1], to, state_sem.at[d - 1])
                copy.wait() if wait else copy.start()

    send_states(False)
    decay, gain = level_factors(rate_ref, var)

    def eight(i, _):
        now = pl.ds(pl.multiple_of(i * 8, 8), 8)
        for cut in column_cuts(columns):
            filter_levels(decay, gain, smooth, cov_ref, now, cut)
        return 0

    lax.fori_loop(0, rows // 8, eight, 0)
    for level in range(levels):
        deliver(level, True)
    send_states(True)
    wipe(True)


def finish(z, vert_rate, owner, rank, place_of, held, table, row_factors, states, chips, capacity, bounds, twin_bounds):
    slabs, rows, columns = z.shape
    early = bounds[0][0]
    state_rows = -(-2 * early // 8) * 8
    chunks = [f32((b - a) * rows + (state_rows if a == early else 0), columns) for a, b in bounds]
    outs = call(
        functools.partial(finish_kernel, chips, capacity, bounds, twin_bounds),
        "finish",
        grid=(VAR,),
        in_specs=[SMEM] * 5
        + [
            pl.BlockSpec((LEV, rows, columns), lambda v: (v, 0, 0)),
            pl.BlockSpec((LEV // GROUP, COLUMNS, rows, GROUP), lambda v: (v, 0, 0, 0)),
            pl.BlockSpec((LEV, 2, 3 * rows), lambda v: (v, 0, 0)),
            pl.BlockSpec((2, LEV, columns), lambda v: (0, v, 0)),
        ],
        out_specs=[pl.BlockSpec((LEV, rows, columns), lambda v: (v, 0, 0))]
        + [ANY] * (1 + len(twin_bounds) + len(bounds) * (chips - 1)),
        out_shape=[f32(*z.shape)]
        + [chunk for chunk in chunks for _ in range(chips - 1)]
        + [f32((b - a) * rows, columns) for a, b in twin_bounds]
        + [f32(capacity, rows, chips * CORES * columns)],
        scratch_shapes=[
            pltpu.VMEM((LEV, rows, columns), jnp.float32),
            pltpu.VMEM((rows, chips * CORES * columns), jnp.float32),
            pltpu.VMEM((chips - 1, state_rows, columns), jnp.float32),
            pltpu.SemaphoreType.DMA((LEV,)),
            pltpu.SemaphoreType.DMA((capacity,)),
            pltpu.SemaphoreType.DMA((chips - 1,)),
        ],
    )(vert_rate, owner, rank, place_of, held, z, table, row_factors, states)
    sent = [outs[1 + k * (chips - 1) : 1 + (k + 1) * (chips - 1)] for k in range(len(bounds))]
    return outs[0], sent, outs[1 + len(bounds) * (chips - 1) : -1], outs[-1]


def finish_early_kernel(first_state, sources, t_ref, r_ref, s_ref, *rest):
    z_refs, done_refs = rest[:sources], rest[sources:]
    rows = z_refs[0].shape[1]
    entries = [(z_ref, n) for z_ref in z_refs for n in range(z_ref.shape[0])]
    e = 0
    for done_ref in done_refs:
        for part in range(0, done_ref.shape[0], rows):
            column = lambda c: t_ref[0, c, :, e : e + 1]
            f_in = s_ref[first_state + e : first_state + e + 1]
            b_in = s_ref[first_state + len(entries) + e : first_state + len(entries) + e + 1]
            z_ref, n = entries[e]
            done_ref[part : part + rows] = finish_tile(z_ref[n], column, r_ref[e], f_in, b_in)
            e += 1


def finish_early(zs, table, row_factors, states, first_state, parts):
    rows, columns = zs[0].shape[1:]
    vmem = pl.BlockSpec(memory_space=pltpu.VMEM)
    return call(
        functools.partial(finish_early_kernel, first_state, len(zs)),
        "finish_early",
        in_specs=[vmem] * (3 + len(zs)),
        out_specs=[vmem] * len(parts),
        out_shape=[f32((b - a) * rows, columns) for a, b in parts],
    )(table, row_factors, states, *zs)


def place_kernel(jobs, tile_ref, *rest):
    slots = rest[: len(jobs)]
    srcs = rest[len(jobs) : 2 * len(jobs)]
    out_ref, held, arrive, leave = rest[-4:]
    rows, columns = held.shape[-2:]
    entries, n = [], 0
    for k, (first, count) in enumerate(jobs):
        for e in range(count):
            entries.append((k, e, first + e, n))
            n += 1

    def read(k, e, at, n):
        return pltpu.make_async_copy(srcs[k].at[pl.ds(e * rows, rows)], held.at[n], arrive.at[n])

    def write(k, e, at, n):
        start = pl.multiple_of(tile_ref[k] * columns, 128)
        return pltpu.make_async_copy(held.at[n], out_ref.at[slots[k][at], :, pl.ds(start, columns)], leave.at[n])

    def each(act):
        for k, e, at, n in entries:

            @pl.when(slots[k][at] >= 0)
            def _():
                act(k, e, at, n)

    def onward(*job):
        read(*job).wait()
        write(*job).start()

    each(lambda *job: read(*job).start())
    each(onward)
    each(lambda *job: write(*job).wait())


def place(out, jobs):
    n = sum(job[3] for job in jobs)
    count = len(jobs)
    return call(
        functools.partial(place_kernel, [(job[2], job[3]) for job in jobs]),
        "place",
        in_specs=[SMEM] * (1 + count) + [ANY] * (count + 1),
        out_specs=ANY,
        out_shape=f32(*out.shape),
        scratch_shapes=[
            pltpu.VMEM((n, out.shape[1], jobs[0][0].shape[1]), jnp.float32),
            pltpu.SemaphoreType.DMA((n,)),
            pltpu.SemaphoreType.DMA((n,)),
        ],
        input_output_aliases={1 + 2 * count: 0},
    )(jnp.stack([job[4] for job in jobs]), *[job[1] for job in jobs], *[job[0] for job in jobs], out)


def scan_rows(states, coef):
    count = lax.axis_size("ty")
    place_y = lax.axis_index("ty")
    f_end, b_start = states[0], states[1]
    f_in = b_in = jnp.zeros_like(f_end)
    stage, bit = 0, 1
    while bit < count:
        upper = (place_y // bit) % 2 == 1
        pairs = [(i, i ^ bit) for i in range(count)]
        p_low, p_high, q_high, own_f, own_bf, own_b = [coef[stage, c][:, None] for c in range(6)]
        low = lambda mine, other: jnp.where(upper, other, mine)
        high = lambda mine, other: jnp.where(upper, mine, other)
        if 2 * bit < count:
            both = states if bit == 1 else jnp.stack([f_end, b_start])
            other_f, other_b = lax.ppermute(both, "ty", pairs)
            f_low, f_high = low(f_end, other_f), high(f_end, other_f)
            b_low, b_high = low(b_start, other_b), high(b_start, other_b)
        else:
            other = lax.ppermute(jnp.where(upper, b_start, f_end), "ty", pairs)
            f_low, b_high = low(f_end, other), high(b_start, other)
        from_above = b_high + q_high * f_low
        f_in = f_in + jnp.where(upper, own_f * f_low, 0.0)
        b_in = b_in + jnp.where(upper, own_bf * f_low, own_b * from_above)
        if 2 * bit < count:
            f_end = f_high + p_high * f_low
            b_start = b_low + p_low * from_above
        stage, bit = stage + 1, 2 * bit
    return jnp.stack([f_in, b_in])


def split(first, last, sizes):
    bounds = []
    for size in [*sizes, last]:
        if first < last:
            bounds.append((first, min(first + size, last)))
            first += size
    return bounds


def as_one(ready, function, *operands, otherwise=None):
    shapes = jax.eval_shape(function, *operands)
    empty = lambda *_: jax.tree.map(lambda x: jnp.zeros(x.shape, x.dtype), shapes)
    return lax.cond(ready, function, otherwise or empty, *operands)


def run(amount, early, increment, vert_rate, zonal_rate, merid_rate, lat_band, slab_owner, lists, v, first_sent, rest_sent):
    slabs, rows, columns = v.shape
    groups = lax.axis_size("tx")
    chips = groups // CORES
    capacity = 2 * slabs // groups
    me = lax.axis_index("tx")
    twin = me ^ 1
    twins = [(i, i ^ 1) for i in range(groups)]
    hop = lambda d: [(i, (i + CORES * d) % groups) for i in range(groups)]
    across = lambda values: [lax.ppermute(a, "tx", hop(d + 1)) for d, a in enumerate(values)]
    pass_on = lambda a: lax.ppermute(a, "tx", twins)
    offsets = range(1, chips)
    source_of = lambda who, d: (who + groups - CORES * d) % groups
    send, recv_slab, recv_slot, held, rank, place_of, step = lists
    ready = step[0] >= 0
    head = first_sent[0].shape[0]
    bounds = split(early, amount, [max(amount - early - capacity // 4 - 1, 1), amount])
    twin_bounds = split(0, capacity, [capacity // 2] * 2)

    first_v = across(first_sent)
    v, rest_sent = vertical_second(increment, vert_rate, slab_owner, send, v, rest_sent, early, head)
    ends = zonal_ends(v, zonal_rate, lat_band)
    own_ends = [ends, *across([ends] * (chips - 1))]
    rest_v = across([gate(a, *own_ends[1:], *first_v) for a in rest_sent])

    def tile(v, own_ends):
        twin_ends = [pass_on(a) for a in own_ends]
        table, table_e, row_factors, row_factors_e, coef = tables(
            zonal_rate, merid_rate, lat_band, recv_slab, own_ends, twin_ends, columns, early
        )
        z, states = zonal(v, table)
        states = scan_rows(states, coef)
        done = finish(
            z, vert_rate, slab_owner, rank, place_of, held, table, row_factors, states, chips, capacity, bounds, twin_bounds
        )
        return done, table_e, row_factors_e

    (covariance, chunks, twin_sent, out), table_e, row_factors_e = as_one(ready, tile, v, own_ends)
    from_twin = [pass_on(a) for a in twin_sent]
    chunks = [across(sent) for sent in chunks]

    out = place(out, [(x, held, i, j - i, twin) for (i, j), x in zip(twin_bounds, from_twin)])
    parts = split(0, early, [capacity // 4] * 4)
    early_z, done, jobs, last_jobs = [], [], [], []
    for d in offsets:
        first_z = zonal(first_v[d - 1], table_e[d - 1 : d])[0]
        early_z.append([first_z, zonal(gate(rest_v[d - 1], first_z, out), table_e[d - 1 : d], head)[0]])
    (a, b), (c, end) = bounds
    for d in offsets:
        here, there = source_of(me, d), source_of(twin, d)
        arrived = gate(chunks[0][d - 1], *[z for zs in early_z for z in zs])
        done = finish_early(early_z[d - 1], table_e[d - 1 : d], row_factors_e, arrived, (b - a) * rows, parts)
        for (i, j), part in zip(parts, done):
            jobs.append((part, recv_slot, i, j - i, here))
            jobs.append((pass_on(part), recv_slot, i, j - i, there))
        last_jobs.append((arrived, recv_slot, a, b - a, here))
        last_jobs.append((pass_on(arrived), recv_slot, a, b - a, there))
    out = place(out, jobs)
    for d in offsets:
        here, there = source_of(me, d), source_of(twin, d)
        arrived = gate(chunks[1][d - 1], out)
        last_jobs.append((arrived, recv_slot, c, end - c, here))
        last_jobs.append((pass_on(arrived), recv_slot, c, end - c, there))
    return covariance, place(out, last_jobs)


def shards(increment, vert_rate, zonal_rate, merid_rate, lat_band, slab_owner):
    slabs = increment.shape[0]
    groups = lax.axis_size("tx")
    capacity = 2 * slabs // groups
    early, head = 15 * capacity // 16, max(3 * capacity // 16, 1)
    ladder = sorted({-(-capacity * n // 16) for n in (21, 22, 32)})
    lists, v, first_sent, rest_sent = vertical_first(
        increment, vert_rate, slab_owner, groups // CORES, capacity, early, head, ladder
    )
    return lax.switch(
        lists[-1][0],
        [functools.partial(run, amount, early) for amount in ladder],
        increment,
        vert_rate,
        zonal_rate,
        merid_rate,
        lat_band,
        slab_owner,
        lists,
        v,
        first_sent,
        rest_sent,
    )


def solution(mesh):
    return jax.shard_map(
        shards,
        mesh=mesh,
        in_specs=(P(None, "ty", "tx"), P(), P(), P(), P(), P()),
        out_specs=(P(None, "ty", "tx"), P("tx", "ty", None)),
        check_vma=False,
    )
```

```python
import functools

import jax
import jax.numpy as jnp
from jax import lax
from jax.experimental import pallas as pl
from jax.experimental.pallas import tpu as pltpu
from jax.sharding import PartitionSpec as P

LEV = 16
VAR = 2
NBANDS = 16
CORES = 2
GROUP = 8
HIGHEST = lax.Precision.HIGHEST
VMEM_LIMIT = 48 * 1024 * 1024
SMEM = pl.BlockSpec(memory_space=pltpu.SMEM)
ANY = pl.BlockSpec(memory_space=pl.ANY)


def call(kernel, name, **how):
    return pl.pallas_call(
        kernel,
        compiler_params=pltpu.CompilerParams(vmem_limit_bytes=VMEM_LIMIT),
        cost_estimate=pl.CostEstimate(flops=0, bytes_accessed=4096, transcendentals=0),
        name=name,
        **how,
    )


def f32(*shape):
    return jax.ShapeDtypeStruct(shape, jnp.float32)


def i32(*shape):
    return jax.ShapeDtypeStruct(shape, jnp.int32)


def gain_of(rates):
    return jnp.sqrt(rates * (2.0 - rates))


def halves(x):
    high = x.astype(jnp.bfloat16)
    low = (x - high.astype(jnp.float32)).astype(jnp.bfloat16)
    return high, low


def exact_dot(a, b):
    return jnp.dot(a, b, precision=HIGHEST, preferred_element_type=jnp.float32)


def iota(shape, dim):
    return lax.broadcasted_iota(jnp.int32, shape, dim)


def select(table, band, shape):
    out = jnp.zeros(shape, jnp.float32)
    for b in range(NBANDS):
        entry = table[b : b + 1, :] if band.shape[1] == 1 else table[:, b : b + 1]
        out = jnp.where(band == b, entry, out)
    return out


def filter_levels(decay, gain, src_ref, dst_ref, rows, cut):
    state, held = None, []
    for level in range(LEV):
        piece = gain[level] * src_ref[level, rows, cut]
        state = piece if state is None else decay[level] * state + piece
        held.append(state)
    state = None
    for level in reversed(range(LEV)):
        piece = gain[level] * held[level]
        state = piece if state is None else decay[level] * state + piece
        dst_ref[level, rows, cut] = state


def level_factors(rate_ref, var):
    rates = [rate_ref[var, level] for level in range(LEV)]
    decay = [1.0 - rate for rate in rates]
    gain = [jnp.sqrt(jnp.full((8, 128), rate * (2.0 - rate), jnp.float32))[:1, :1] for rate in rates]
    return decay, gain


def column_cuts(columns):
    width = 384 if columns % 384 == 0 else 128
    return [slice(start, start + width) for start in range(0, columns, width)]


def write_lists(chips, capacity, head, ladder, owner_ref, send_ref, recv_ref, slot_ref, held_ref, rank_ref, place_ref, step_ref, counts):
    slabs = owner_ref.shape[0]
    most = ladder[-1]
    me = lax.axis_index("tx")
    chip = lax.div(me, CORES)
    for c in range(chips * (1 + CORES)):
        counts[c] = 0
    for e in range((chips - 1) * most):
        send_ref[e] = 0
    for e in range(most):
        recv_ref[e] = 0
        slot_ref[e] = -1
    for e in range(capacity):
        held_ref[e] = -1

    def one(s, _):
        owner = owner_ref[s]
        its_chip = lax.div(owner, CORES)
        rank = counts[its_chip]
        slot = counts[chips + owner]
        counts[its_chip] = rank + 1
        counts[chips + owner] = slot + 1
        rank_ref[s] = rank
        place_ref[s] = slot
        away = lax.rem(its_chip + chips - chip, chips)
        send_ref[jnp.where(away == 0, (chips - 1) * most, (away - 1) * most + rank)] = s
        here = jnp.where(away == 0, rank, most)
        mine = owner == me
        recv_ref[here] = s
        slot_ref[here] = jnp.where(mine, slot, -1)
        held_ref[jnp.where(mine, slot, capacity)] = slot
        return 0

    lax.fori_loop(0, LEV, one, 0, unroll=4)
    for c in range(chips):
        counts[c] = jnp.maximum(counts[c], head)
    lax.fori_loop(LEV, slabs, one, 0, unroll=4)
    needed = counts[0]
    for c in range(1, chips):
        needed = jnp.maximum(needed, counts[c])
    step = jnp.int32(0)
    for amount in ladder[:-1]:
        step = step + jnp.where(needed > amount, 1, 0)
    step_ref[0] = step


def first_rows(e, part):
    return e * part


def rest_row(e, row, rows, part, head):
    return e * (rows - part) + row - part if e < head else head * (rows - part) + (e - head) * rows + row


def filter_block(rate_ref, var, x_ref, v_ref):
    decay, gain = level_factors(rate_ref, var)

    def eight(i, _):
        now = pl.ds(pl.multiple_of(i * 8, 8), 8)
        for cut in column_cuts(x_ref.shape[-1]):
            filter_levels(decay, gain, x_ref, v_ref, now, cut)
        return 0

    lax.fori_loop(0, x_ref.shape[1] // 8, eight, 0)


def first_kernel(chips, capacity, early, head, ladder, rows, rate_ref, owner_ref, x_ref, *rest):
    lists, v_ref, first_refs, rest_refs = rest[:7], rest[7], rest[8 : 7 + chips], rest[7 + chips : 6 + 2 * chips]
    counts, sem = rest[-2:]
    part = x_ref.shape[1]
    write_lists(chips, capacity, head, ladder, owner_ref, *lists, counts)
    filter_block(rate_ref, 0, x_ref, v_ref)
    for wait in (False, True):
        for d in range(chips - 1):
            for e in range(early):
                slab = lists[0][d * ladder[-1] + e]
                if e < head:
                    to = first_refs[d].at[pl.ds(first_rows(e, part), part)]
                else:
                    to = rest_refs[d].at[pl.ds(rest_row(e, 0, rows, part, head), part)]

                @pl.when(slab < LEV)
                def _():
                    copy = pltpu.make_async_copy(v_ref.at[slab], to, sem.at[d, e])
                    copy.wait() if wait else copy.start()


def second_kernel(chips, most, early, head, rows, rate_ref, x_ref, send_ref, *rest):
    v_ref, rest_refs, sem = rest[chips], rest[1 + chips : 2 * chips], rest[-1]
    part = x_ref.shape[1]
    parts = rows // part
    step, steps = pl.program_id(0), pl.num_programs(0)
    filter_block(rate_ref, lax.div(step + 1, parts), x_ref, v_ref)

    def copies(step, wait):
        var, which = lax.div(step + 1, parts), lax.rem(step + 1, parts)
        for d in range(chips - 1):
            for e in range(early):
                slab = send_ref[d * most + e]
                wanted = lax.div(slab, LEV) == var
                row = rest_row(e, 0, rows, part, head) + which * part
                if e < head:
                    wanted = jnp.logical_and(wanted, which > 0)

                @pl.when(wanted)
                def _():
                    to = rest_refs[d].at[pl.ds(pl.multiple_of(row, 8), part)]
                    copy = pltpu.make_async_copy(v_ref.at[lax.rem(slab, LEV)], to, sem.at[step, d, e])
                    copy.wait() if wait else copy.start()

    copies(step, False)

    @pl.when(step > 0)
    def _():
        copies(step - 1, True)

    @pl.when(step == steps - 1)
    def _():
        copies(step, True)


def vertical_first(increment, vert_rate, slab_owner, chips, capacity, early, head, part, ladder):
    slabs, rows, columns = increment.shape
    most = ladder[-1]
    spec = pl.BlockSpec((LEV, part, columns), lambda r: (0, 0, 0))
    lists = [(chips - 1) * most + 1, most + 1, most + 1, capacity + 1, slabs, slabs, 1]
    rest_rows = head * (rows - part) + (early - head) * rows
    outs = call(
        functools.partial(first_kernel, chips, capacity, early, head, ladder, rows),
        "vertical_first",
        grid=(1,),
        in_specs=[SMEM, SMEM, spec],
        out_specs=[SMEM] * 7 + [spec] + [ANY] * (2 * chips - 2),
        out_shape=[i32(n) for n in lists]
        + [f32(*increment.shape)]
        + [f32(head * part, columns)] * (chips - 1)
        + [f32(rest_rows, columns)] * (chips - 1),
        scratch_shapes=[
            pltpu.SMEM((chips * (1 + CORES),), jnp.int32),
            pltpu.SemaphoreType.DMA((chips - 1, early)),
        ],
    )(vert_rate, slab_owner, increment)
    return outs[:7], outs[7], outs[8 : 7 + chips], outs[7 + chips :]


def vertical_second(increment, vert_rate, send, v, rest_sent, early, head, part, most):
    slabs, rows, columns = increment.shape
    chips = 1 + len(rest_sent)
    parts = rows // part
    steps = VAR * parts - 1
    spec = pl.BlockSpec((LEV, part, columns), lambda n: (lax.div(n + 1, parts), lax.rem(n + 1, parts), 0))
    outs = call(
        functools.partial(second_kernel, chips, most, early, head, rows),
        "vertical_second",
        grid=(steps,),
        in_specs=[SMEM, spec, SMEM] + [ANY] * chips,
        out_specs=[spec] + [ANY] * (chips - 1),
        out_shape=[f32(*v.shape)] + [f32(*a.shape) for a in rest_sent],
        scratch_shapes=[pltpu.SemaphoreType.DMA((steps, chips - 1, early))],
        input_output_aliases={3 + n: n for n in range(chips)},
    )(vert_rate, increment, send, v, *rest_sent)
    return outs[0], outs[1:]


def ends_kernel(band_ref, zonal_ref, v_ref, ends_ref, la_ref):
    levels, rows, columns = v_ref.shape
    var = pl.program_id(0)

    @pl.when(var == 0)
    def _():
        first = lax.axis_index("ty") * rows

        def fetch(r, _):
            la_ref[pl.ds(r, 1), :] = zonal_ref[pl.ds(band_ref[first + r], 1), :]
            return 0

        lax.fori_loop(0, rows, fetch, 0)
        la_ref[...] = jnp.log1p(-la_ref[...])
        ends_ref[...] = jnp.zeros(ends_ref.shape, jnp.float32)

    lane = iota((1, 128), 1).astype(jnp.float32)
    slabs = la_ref.shape[1]
    slab_lane = iota((8, slabs), 1)
    blocks = columns // 128

    def row_sums(parts):
        high, low = halves(jnp.concatenate(parts, axis=0))
        ones = jnp.ones((128, 128), jnp.bfloat16)
        dot = functools.partial(jnp.dot, preferred_element_type=jnp.float32)
        return dot(high, ones) + dot(low, ones)

    def eight(i, _):
        now = pl.ds(pl.multiple_of(i * 8, 8), 8)
        la_rows = jnp.where(var == 1, la_ref[now, LEV:], la_ref[now, :LEV])
        whole_rows = jnp.exp(la_rows * 128.0)
        rights, lefts = [], []
        for level in range(levels):
            la = jnp.broadcast_to(la_rows[:, level : level + 1], (8, 128))
            whole = jnp.broadcast_to(whole_rows[:, level : level + 1], (8, 128))
            pieces = [v_ref[level, now, b * 128 : (b + 1) * 128] for b in range(blocks)]
            right, left = pieces[0], pieces[-1]
            for b in range(1, blocks):
                right = whole * right + pieces[b]
                left = whole * left + pieces[blocks - 1 - b]
            rights.append(right * jnp.exp(la * (127.0 - lane)))
            lefts.append(left * jnp.exp(la * lane))
        right, left = row_sums(rights), row_sums(lefts)
        right_ends, left_ends = ends_ref[0, now, :], ends_ref[1, now, :]
        for level in range(levels):
            here = slab_lane == var * LEV + level
            right_ends = jnp.where(here, right[level * 8 : (level + 1) * 8, :slabs], right_ends)
            left_ends = jnp.where(here, left[level * 8 : (level + 1) * 8, :slabs], left_ends)
        ends_ref[0, now, :] = right_ends
        ends_ref[1, now, :] = left_ends
        return 0

    lax.fori_loop(0, rows // 8, eight, 0, unroll=2 if rows % 16 == 0 else 1)


def zonal_ends(v, zonal_rate, lat_band):
    slabs, rows, columns = v.shape
    return call(
        ends_kernel,
        "ends",
        grid=(VAR,),
        in_specs=[
            SMEM,
            pl.BlockSpec(zonal_rate.shape, lambda v: (0, 0)),
            pl.BlockSpec((LEV, rows, columns), lambda v: (v, 0, 0)),
        ],
        out_specs=pl.BlockSpec((2, rows, slabs), lambda v: (0, 0, 0)),
        out_shape=f32(2, rows, slabs),
        scratch_shapes=[pltpu.VMEM((rows, slabs), jnp.float32)],
    )(lat_band, zonal_rate, v)


def gate_kernel(*refs):
    pass


def gate(value, *after):
    return call(
        gate_kernel,
        "gate",
        in_specs=[ANY] * (1 + len(after)),
        out_specs=ANY,
        out_shape=jax.ShapeDtypeStruct(value.shape, value.dtype),
        input_output_aliases={0: 0},
    )(value, *after)


COLUMNS = 8


def tables_kernel(chips, devices, early, width, recv_ref, zonal_ref, merid_ref, merid_t_ref, band_ref, own_band_ref, row_ref, *rest):
    own_ends, twin_ends = rest[:chips], rest[chips : 2 * chips]
    t_ref, te_ref, r_ref, re_ref, coef_ref, hold = rest[2 * chips :]
    rows, slabs = own_ends[0].shape[1:]
    groups = chips * CORES
    me, place_y = lax.axis_index("tx"), lax.axis_index("ty")

    k, m = iota((rows, rows), 0), iota((rows, rows), 1)
    below, above = (k >= m).astype(jnp.float32), (k <= m).astype(jnp.float32)
    own_band = own_band_ref[...]
    la = jnp.log1p(-select(zonal_ref[...], own_band, (rows, slabs)))

    def tables_of(rates):
        log_decay = jnp.log1p(-rates)
        inclusive = exact_dot(below, log_decay)
        exclusive = inclusive - log_decay
        gains = gain_of(rates)
        sums = exact_dot(above, gains * jnp.exp(inclusive + exclusive))
        return inclusive, exclusive, gains, sums

    inclusive, exclusive, gains, sums = tables_of(select(merid_ref[...], own_band, (rows, slabs)))
    whole = jnp.exp(inclusive[rows - 1 :, :])
    before = gains * jnp.exp(-inclusive)
    after = jnp.exp(-exclusive)
    meridional = [whole * before, before * sums, after * sums, after, whole * after]

    tile_decay = jnp.exp(la * float(width))
    my_chip, my_core = lax.div(me, CORES), lax.rem(me, CORES)

    def ends_of(t, side):
        away = lax.rem(my_chip + chips - t // CORES, chips)
        out = jnp.zeros((rows, slabs), jnp.float32)
        for d in range(chips):
            value = jnp.where(my_core == t % CORES, own_ends[d][side], twin_ends[d][side])
            out = jnp.where(away == d, value, out)
        return out

    from_left = [jnp.zeros((rows, slabs), jnp.float32)]
    for t in range(groups):
        from_left.append(ends_of(t, 0) + tile_decay * from_left[-1])
    from_right = [-jnp.exp(la) * from_left[-1]]
    for t in reversed(range(1, groups)):
        from_right.append(ends_of(t, 1) + tile_decay * from_right[-1])
    from_right = from_right[::-1]

    def entering(tile):
        left = right = jnp.zeros((rows, slabs), jnp.float32)
        for t in range(groups):
            left = jnp.where(tile == t, from_left[t], left)
            right = jnp.where(tile == t, from_right[t], right)
        return left, right

    for c, table in enumerate([la, *entering(me), *meridional]):
        for g in range(slabs // GROUP):
            t_ref[g, c] = table[:, g * GROUP : (g + 1) * GROUP]
    slab, entry = iota((slabs, early), 0), iota((slabs, early), 1)
    hit = jnp.zeros((slabs, early), jnp.float32)
    for e in range(early):
        hit = jnp.where(jnp.logical_and(entry == e, slab == recv_ref[e]), 1.0, hit)
    common = [exact_dot(table, hit) for table in [la, *meridional]]
    for d in range(1, chips):
        left, right = entering(lax.rem(me + groups - CORES * d, groups))
        for c, table in enumerate([common[0], exact_dot(left, hit), exact_dot(right, hit), *common[1:]]):
            te_ref[d - 1, c] = table

    wide = 3 * rows
    k, m = iota((rows, wide), 0), iota((rows, wide), 1)
    m = m - jnp.where(m >= 2 * rows, 2 * rows, jnp.where(m >= rows, rows, 0))
    upto, onward = (k <= m).astype(jnp.float32), (k >= m).astype(jnp.float32)
    band_row = row_ref[...]
    rates = select(merid_t_ref[...], band_row, (slabs, wide))
    log_row = jnp.log1p(-rates[:, :rows])
    inclusive_row = exact_dot(log_row, upto)
    here = inclusive_row[:, :rows]
    sums_row = exact_dot(gain_of(rates[:, :rows]) * jnp.exp(2.0 * here - log_row), onward)
    before_row = gain_of(rates) * jnp.exp(-inclusive_row)
    after_row = before_row * sums_row
    for s in range(slabs):
        r_ref[s, 0:1] = before_row[s : s + 1]
        r_ref[s, 1:2] = after_row[s : s + 1]
    for e in range(early):
        re_ref[e] = r_ref[recv_ref[e]]

    decay, cross = [], []
    for n in range(devices):
        band = band_ref[n * rows : (n + 1) * rows]
        inclusive, _, _, sums = tables_of(select(merid_ref[...], band, (rows, slabs)))
        decay.append(jnp.exp(inclusive[rows - 1 :, :]))
        cross.append(sums[0:1, :])
    decay, cross = jnp.concatenate(decay, axis=0), jnp.concatenate(cross, axis=0)
    device = iota((devices, slabs), 0)
    own_f, own_bf, own_b = jnp.ones_like(decay), jnp.zeros_like(decay), jnp.ones_like(decay)
    stage, bit = 0, 1
    while bit < devices:
        upper = lax.rem(lax.div(device, bit), 2) == 1
        swap = lambda a: jnp.concatenate([a[n ^ bit : (n ^ bit) + 1] for n in range(devices)], axis=0)
        other_decay, other_cross = swap(decay), swap(cross)
        d_low, d_high = jnp.where(upper, other_decay, decay), jnp.where(upper, decay, other_decay)
        c_low, c_high = jnp.where(upper, other_cross, cross), jnp.where(upper, cross, other_cross)
        for c, table in enumerate([d_low, d_high, c_high, own_f, own_bf, own_b]):
            hold[...] = table
            coef_ref[stage, c : c + 1] = hold[pl.ds(place_y, 1), :]
        own_bf = jnp.where(upper, own_bf * d_low, own_bf + own_b * c_high * d_low)
        own_f = jnp.where(upper, own_f * d_low, own_f)
        own_b = jnp.where(upper, own_b, own_b * d_high)
        decay, cross = d_low * d_high, c_low + d_low * d_low * c_high
        stage, bit = stage + 1, 2 * bit


def tables(zonal_rate, merid_rate, lat_band, recv_slab, own_ends, twin_ends, columns, early):
    chips = len(own_ends)
    devices = lax.axis_size("ty")
    _, rows, slabs = own_ends[0].shape
    stages = (devices - 1).bit_length()
    own = lax.dynamic_slice_in_dim(lat_band, lax.axis_index("ty") * rows, rows)
    vmem = pl.BlockSpec(memory_space=pltpu.VMEM)
    return call(
        functools.partial(tables_kernel, chips, devices, early, columns),
        "tables",
        in_specs=[SMEM] + [vmem] * (6 + 2 * chips),
        out_specs=[vmem] * 5,
        out_shape=[
            f32(slabs // GROUP, COLUMNS, rows, GROUP),
            f32(chips - 1, COLUMNS, rows, early),
            f32(slabs, 2, 3 * rows),
            f32(early, 2, 3 * rows),
            f32(stages, 6, slabs),
        ],
        scratch_shapes=[pltpu.VMEM((devices, slabs), jnp.float32)],
    )(
        recv_slab,
        zonal_rate,
        merid_rate,
        merid_rate.T,
        lat_band[:, None],
        own[:, None],
        jnp.tile(own, 3)[None, :],
        *own_ends,
        *twin_ends,
    )


def zonal_tile(v, la, left, right, block):
    rows, columns = v.shape
    half = block // 2
    blocks = columns // block
    j, i = iota((block, block), 0), iota((block, block), 1)
    upto = jnp.where(j <= i, 1.0, 0.0).astype(jnp.bfloat16)
    onward = jnp.where(j >= i, 1.0, 0.0).astype(jnp.bfloat16)
    power = la * (iota((1, block), 1) - half).astype(jnp.float32)
    up, down = jnp.exp(power), jnp.exp(-power)
    value = [v[:, b * block : (b + 1) * block] for b in range(blocks)]

    def totals(scale, ones):
        high, low = halves(jnp.concatenate([x * scale for x in value], axis=0))
        dot = functools.partial(jnp.dot, preferred_element_type=jnp.float32)
        total = dot(high, ones) + dot(low, ones)
        return [total[b * rows : (b + 1) * rows] for b in range(blocks)]

    enter = jnp.exp(la * (half + 1.0))
    state, rising = left, []
    for total in totals(down, upto):
        now = up * (total + enter * state)
        state = now[:, block - 1 :]
        rising.append(now)
    enter = jnp.exp(la * float(half))
    state, result = right, [None] * blocks
    parts = totals(up, onward)
    for b in reversed(range(blocks)):
        now = down * (parts[b] + enter * state)
        state = now[:, :1]
        result[b] = rising[b] + now - value[b]
    return result


def zonal_kernel(v_ref, t_ref, z_ref, o_ref):
    for s in range(v_ref.shape[0]):
        block = 256 if v_ref.shape[-1] % 256 == 0 else 128
        column = lambda c: jnp.broadcast_to(t_ref[0, c, :, s : s + 1], (t_ref.shape[2], block))
        result = zonal_tile(v_ref[s], column(0), column(1), column(2), block)
        for side in range(2):
            weight = column(3 + side)
            for b, z in enumerate(result):
                o_ref[side, s : s + 1, b * block : (b + 1) * block] = jnp.sum(z * weight, axis=0, keepdims=True)
        for b, z in enumerate(result):
            z_ref[s, :, b * block : (b + 1) * block] = z


def zonal(v, table):
    slabs, rows, columns = v.shape
    return call(
        zonal_kernel,
        "zonal",
        grid=(slabs // GROUP,),
        in_specs=[
            pl.BlockSpec((GROUP, rows, columns), lambda s: (s, 0, 0)),
            pl.BlockSpec((1, *table.shape[1:]), lambda s: (s, 0, 0, 0)),
        ],
        out_specs=[
            pl.BlockSpec((GROUP, rows, columns), lambda s: (s, 0, 0)),
            pl.BlockSpec((2, GROUP, columns), lambda s: (0, s, 0)),
        ],
        out_shape=[f32(*v.shape), f32(2, slabs, columns)],
    )(v, table)


def zonal_rows_kernel(pieces, v_ref, t_ref, z_ref):
    block = 256 if v_ref.shape[-1] % 256 == 0 else 128
    for at, e, row, count in pieces:
        column = lambda c: jnp.broadcast_to(t_ref[0, c, row : row + count, e : e + 1], (count, block))
        result = zonal_tile(v_ref[at : at + count], column(0), column(1), column(2), block)
        for b, z in enumerate(result):
            z_ref[at : at + count, b * block : (b + 1) * block] = z


def zonal_rows(v, table, pieces):
    vmem = pl.BlockSpec(memory_space=pltpu.VMEM)
    return call(
        functools.partial(zonal_rows_kernel, pieces),
        "zonal_rows",
        in_specs=[vmem, vmem],
        out_specs=vmem,
        out_shape=f32(*v.shape),
    )(v, table)


def finish_tile(z, column, row_factors, f_in, b_in):
    rows = z.shape[0]
    wide = 3 * rows
    i, r = iota((rows, wide), 0), iota((rows, wide), 1)
    third = r >= 2 * rows
    r = r - jnp.where(third, 2 * rows, jnp.where(r >= rows, rows, 0))
    a, c = column(5), column(6)
    matrix = jnp.where(i >= r, a * row_factors[0:1], c * row_factors[1:2])
    high = matrix.astype(jnp.bfloat16)
    low = (matrix - high.astype(jnp.float32)).astype(jnp.bfloat16)
    matrix = jnp.where(third, low.astype(jnp.float32), high.astype(jnp.float32)).astype(jnp.bfloat16)
    z_high, z_low = halves(z)
    dot = functools.partial(jnp.dot, preferred_element_type=jnp.float32)
    if rows % 16 == 0:
        result = dot(matrix, jnp.concatenate([z_high, z_low, z_high], axis=0))
    else:
        result = dot(matrix[:, :rows], z_high) + dot(matrix[:, rows : 2 * rows], z_low)
        result = result + dot(matrix[:, 2 * rows :], z_high)
    return result + a * f_in + column(7) * b_in


def finish_kernel(chips, capacity, bounds, twin_bounds, rate_ref, owner_ref, rank_ref, place_ref, held_ref, z_ref, t_ref, r_ref, s_ref, *rest):
    cov_ref = rest[0]
    chunk_refs = [rest[1 + k * (chips - 1) : 1 + (k + 1) * (chips - 1)] for k in range(len(bounds))]
    rest = rest[1 + len(bounds) * (chips - 1) :]
    twin_refs, rest = rest[: len(twin_bounds)], rest[len(twin_bounds) :]
    out_ref, smooth, blank, early_states, sem, wipe_sem, state_sem = rest
    early = bounds[0][0]
    levels, rows, columns = z_ref.shape
    var = pl.program_id(0)
    me = lax.axis_index("tx")
    my_chip = lax.div(me, CORES)
    first = pl.multiple_of(me * columns, 128)

    def wipe(wait):
        for e in range(capacity):

            @pl.when(jnp.logical_and(var == 0, held_ref[e] < 0))
            def _():
                copy = pltpu.make_async_copy(blank, out_ref.at[e], wipe_sem.at[e])
                copy.wait() if wait else copy.start()

    @pl.when(var == 0)
    def _():
        blank[...] = jnp.zeros(blank.shape, jnp.float32)
        early_states[...] = jnp.zeros(early_states.shape, jnp.float32)

    wipe(False)

    def deliver(level, wait):
        slab = var * LEV + level
        owner, rank, slot = owner_ref[slab], rank_ref[slab], place_ref[slab]
        away = lax.rem(lax.div(owner, CORES) + chips - my_chip, chips)

        def move(condition, to):
            @pl.when(condition)
            def _():
                copy = pltpu.make_async_copy(smooth.at[level], to(), sem.at[level])
                copy.wait() if wait else copy.start()

        for d in range(1, chips):
            there = away == d
            for (a, b), refs in zip(bounds, chunk_refs):
                within = jnp.logical_and(there, jnp.logical_and(rank >= a, rank < b))
                at = pl.multiple_of((rank - a) * rows, 8)
                move(within, lambda: refs[d - 1].at[pl.ds(at, rows)])
            if not wait:

                @pl.when(jnp.logical_and(there, rank < early))
                def _():
                    early_states[d - 1, pl.ds(rank, 1), :] = s_ref[0, level : level + 1, :]
                    early_states[d - 1, pl.ds(early + rank, 1), :] = s_ref[1, level : level + 1, :]
        move(owner == me, lambda: out_ref.at[slot, :, pl.ds(first, columns)])
        for (a, b), ref in zip(twin_bounds, twin_refs):
            within = jnp.logical_and(slot >= a, slot < b)
            at = pl.multiple_of((slot - a) * rows, 8)
            move(jnp.logical_and(jnp.logical_and(away == 0, owner != me), within), lambda: ref.at[pl.ds(at, rows)])

    for level in range(levels):
        column = lambda c: t_ref[level // GROUP, c, :, level % GROUP : level % GROUP + 1]
        states = s_ref[:, level, :]
        smooth[level] = finish_tile(z_ref[level], column, r_ref[level], states[0:1], states[1:2])
        deliver(level, False)

    def send_states(wait):
        for d in range(1, chips):

            @pl.when(var == VAR - 1)
            def _():
                to = chunk_refs[0][d - 1].at[pl.ds((bounds[0][1] - early) * rows, early_states.shape[1])]
                copy = pltpu.make_async_copy(early_states.at[d - 1], to, state_sem.at[d - 1])
                copy.wait() if wait else copy.start()

    send_states(False)
    decay, gain = level_factors(rate_ref, var)

    def eight(i, _):
        now = pl.ds(pl.multiple_of(i * 8, 8), 8)
        for cut in column_cuts(columns):
            filter_levels(decay, gain, smooth, cov_ref, now, cut)
        return 0

    lax.fori_loop(0, rows // 8, eight, 0)
    for level in range(levels):
        deliver(level, True)
    send_states(True)
    wipe(True)


def finish(z, vert_rate, owner, rank, place_of, held, table, row_factors, states, chips, capacity, bounds, twin_bounds):
    slabs, rows, columns = z.shape
    early = bounds[0][0]
    state_rows = -(-2 * early // 8) * 8
    chunks = [f32((b - a) * rows + (state_rows if a == early else 0), columns) for a, b in bounds]
    outs = call(
        functools.partial(finish_kernel, chips, capacity, bounds, twin_bounds),
        "finish",
        grid=(VAR,),
        in_specs=[SMEM] * 5
        + [
            pl.BlockSpec((LEV, rows, columns), lambda v: (v, 0, 0)),
            pl.BlockSpec((LEV // GROUP, COLUMNS, rows, GROUP), lambda v: (v, 0, 0, 0)),
            pl.BlockSpec((LEV, 2, 3 * rows), lambda v: (v, 0, 0)),
            pl.BlockSpec((2, LEV, columns), lambda v: (0, v, 0)),
        ],
        out_specs=[pl.BlockSpec((LEV, rows, columns), lambda v: (v, 0, 0))]
        + [ANY] * (1 + len(twin_bounds) + len(bounds) * (chips - 1)),
        out_shape=[f32(*z.shape)]
        + [chunk for chunk in chunks for _ in range(chips - 1)]
        + [f32((b - a) * rows, columns) for a, b in twin_bounds]
        + [f32(capacity, rows, chips * CORES * columns)],
        scratch_shapes=[
            pltpu.VMEM((LEV, rows, columns), jnp.float32),
            pltpu.VMEM((rows, chips * CORES * columns), jnp.float32),
            pltpu.VMEM((chips - 1, state_rows, columns), jnp.float32),
            pltpu.SemaphoreType.DMA((LEV,)),
            pltpu.SemaphoreType.DMA((capacity,)),
            pltpu.SemaphoreType.DMA((chips - 1,)),
        ],
    )(vert_rate, owner, rank, place_of, held, z, table, row_factors, states)
    sent = [outs[1 + k * (chips - 1) : 1 + (k + 1) * (chips - 1)] for k in range(len(bounds))]
    return outs[0], sent, outs[1 + len(bounds) * (chips - 1) : -1], outs[-1]


def finish_early_kernel(first_state, early, head, part, rows, t_ref, r_ref, s_ref, first_ref, rest_ref, *done_refs):
    e = 0
    for done_ref in done_refs:
        for at in range(0, done_ref.shape[0], rows):
            if e >= early:
                done_ref[at : at + rows] = s_ref[(e - early) * rows : (e - early + 1) * rows]
                e += 1
                continue
            column = lambda c: t_ref[0, c, :, e : e + 1]
            f_in = s_ref[first_state + e : first_state + e + 1]
            b_in = s_ref[first_state + early + e : first_state + early + e + 1]
            if e >= head:
                row = rest_row(e, 0, rows, part, head)
                z = rest_ref[row : row + rows]
            else:
                z = first_ref[first_rows(e, part) : first_rows(e, part) + part]
                if part < rows:
                    row = rest_row(e, part, rows, part, head)
                    z = jnp.concatenate([z, rest_ref[row : row + rows - part]], axis=0)
            done_ref[at : at + rows] = finish_tile(z, column, r_ref[e], f_in, b_in)
            e += 1


def finish_early(first_z, rest_z, table, row_factors, states, first_state, parts, head, part):
    rows, early = table.shape[2:]
    vmem = pl.BlockSpec(memory_space=pltpu.VMEM)
    return call(
        functools.partial(finish_early_kernel, first_state, early, head, part, rows),
        "finish_early",
        in_specs=[vmem] * 5,
        out_specs=[vmem] * len(parts),
        out_shape=[f32((b - a) * rows, states.shape[1]) for a, b in parts],
    )(table, row_factors, states, first_z, rest_z)


def place_kernel(jobs, tile_ref, *rest):
    slots = rest[: len(jobs)]
    srcs = rest[len(jobs) : 2 * len(jobs)]
    out_ref, held, arrive, leave = rest[-4:]
    rows, columns = held.shape[-2:]
    entries, n = [], 0
    for k, (first, count) in enumerate(jobs):
        for e in range(count):
            entries.append((k, e, first + e, n))
            n += 1

    def read(k, e, at, n):
        return pltpu.make_async_copy(srcs[k].at[pl.ds(e * rows, rows)], held.at[n], arrive.at[n])

    def write(k, e, at, n):
        start = pl.multiple_of(tile_ref[k] * columns, 128)
        return pltpu.make_async_copy(held.at[n], out_ref.at[slots[k][at], :, pl.ds(start, columns)], leave.at[n])

    def each(act):
        for k, e, at, n in entries:

            @pl.when(slots[k][at] >= 0)
            def _():
                act(k, e, at, n)

    def onward(*job):
        read(*job).wait()
        write(*job).start()

    each(lambda *job: read(*job).start())
    each(onward)
    each(lambda *job: write(*job).wait())


def place(out, jobs):
    n = sum(job[3] for job in jobs)
    count = len(jobs)
    return call(
        functools.partial(place_kernel, [(job[2], job[3]) for job in jobs]),
        "place",
        in_specs=[SMEM] * (1 + count) + [ANY] * (count + 1),
        out_specs=ANY,
        out_shape=f32(*out.shape),
        scratch_shapes=[
            pltpu.VMEM((n, out.shape[1], jobs[0][0].shape[1]), jnp.float32),
            pltpu.SemaphoreType.DMA((n,)),
            pltpu.SemaphoreType.DMA((n,)),
        ],
        input_output_aliases={1 + 2 * count: 0},
    )(jnp.stack([job[4] for job in jobs]), *[job[1] for job in jobs], *[job[0] for job in jobs], out)


def scan_rows(states, coef):
    count = lax.axis_size("ty")
    place_y = lax.axis_index("ty")
    f_end, b_start = states[0], states[1]
    f_in = b_in = jnp.zeros_like(f_end)
    stage, bit = 0, 1
    while bit < count:
        upper = (place_y // bit) % 2 == 1
        pairs = [(i, i ^ bit) for i in range(count)]
        p_low, p_high, q_high, own_f, own_bf, own_b = [coef[stage, c][:, None] for c in range(6)]
        low = lambda mine, other: jnp.where(upper, other, mine)
        high = lambda mine, other: jnp.where(upper, mine, other)
        if 2 * bit < count:
            both = states if bit == 1 else jnp.stack([f_end, b_start])
            other_f, other_b = lax.ppermute(both, "ty", pairs)
            f_low, f_high = low(f_end, other_f), high(f_end, other_f)
            b_low, b_high = low(b_start, other_b), high(b_start, other_b)
        else:
            other = lax.ppermute(jnp.where(upper, b_start, f_end), "ty", pairs)
            f_low, b_high = low(f_end, other), high(b_start, other)
        from_above = b_high + q_high * f_low
        f_in = f_in + jnp.where(upper, own_f * f_low, 0.0)
        b_in = b_in + jnp.where(upper, own_bf * f_low, own_b * from_above)
        if 2 * bit < count:
            f_end = f_high + p_high * f_low
            b_start = b_low + p_low * from_above
        stage, bit = stage + 1, 2 * bit
    return jnp.stack([f_in, b_in])


def split(first, last, sizes):
    bounds = []
    for size in [*sizes, last]:
        if first < last:
            bounds.append((first, min(first + size, last)))
            first += size
    return bounds


def as_one(ready, function, *operands, otherwise=None):
    shapes = jax.eval_shape(function, *operands)
    empty = lambda *_: jax.tree.map(lambda x: jnp.zeros(x.shape, x.dtype), shapes)
    return lax.cond(ready, function, otherwise or empty, *operands)


def run(amount, early, head, part, most, increment, vert_rate, zonal_rate, merid_rate, lat_band, slab_owner, lists, v, first_sent, rest_sent):
    slabs, rows, columns = v.shape
    groups = lax.axis_size("tx")
    chips = groups // CORES
    capacity = 2 * slabs // groups
    me = lax.axis_index("tx")
    twin = me ^ 1
    twins = [(i, i ^ 1) for i in range(groups)]
    hop = lambda d: [(i, (i + CORES * d) % groups) for i in range(groups)]
    across = lambda values: [lax.ppermute(a, "tx", hop(d + 1)) for d, a in enumerate(values)]
    pass_on = lambda a: lax.ppermute(a, "tx", twins)
    offsets = range(1, chips)
    source_of = lambda who, d: (who + groups - CORES * d) % groups
    send, recv_slab, recv_slot, held, rank, place_of, step = lists
    ready = step[0] >= 0
    bounds = split(early, amount, [max(amount - early - capacity // 4 - 1, 1), amount])
    twin_bounds = split(0, capacity, [capacity // 2] * 2)

    first_v = across(first_sent)
    v, rest_sent = vertical_second(increment, vert_rate, send, v, rest_sent, early, head, part, most)
    ends = zonal_ends(v, zonal_rate, lat_band)
    own_ends = [ends, *across([ends] * (chips - 1))]
    rest_v = across([gate(a, *own_ends[1:], *first_v) for a in rest_sent])

    def tile(v, own_ends):
        twin_ends = [pass_on(a) for a in own_ends]
        table, table_e, row_factors, row_factors_e, coef = tables(
            zonal_rate, merid_rate, lat_band, recv_slab, own_ends, twin_ends, columns, early
        )
        z, states = zonal(v, table)
        states = scan_rows(states, coef)
        done = finish(
            z, vert_rate, slab_owner, rank, place_of, held, table, row_factors, states, chips, capacity, bounds, twin_bounds
        )
        return done, table_e, row_factors_e

    (covariance, chunks, twin_sent, out), table_e, row_factors_e = as_one(ready, tile, v, own_ends)
    from_twin = [pass_on(a) for a in twin_sent]
    chunks = [across(sent) for sent in chunks]

    out = place(out, [(x, held, i, j - i, twin) for (i, j), x in zip(twin_bounds, from_twin)])
    parts = split(0, min(capacity, bounds[0][1]), [capacity // 4] * 4)
    first_pieces = [(first_rows(e, part), e, 0, part) for e in range(head)]
    rest_pieces = [(rest_row(e, part, rows, part, head), e, part, rows - part) for e in range(head) if part < rows]
    rest_pieces += [(rest_row(e, 0, rows, part, head), e, 0, rows) for e in range(head, early)]
    early_z, jobs, next_jobs, last_jobs = [], [], [], []
    for d in offsets:
        first_z = zonal_rows(first_v[d - 1], table_e[d - 1 : d], first_pieces)
        early_z.append([first_z, zonal_rows(gate(rest_v[d - 1], first_z, out), table_e[d - 1 : d], rest_pieces)])
    (a, b), (c, end) = bounds
    for d in offsets:
        here, there = source_of(me, d), source_of(twin, d)
        arrived = gate(chunks[0][d - 1], *[z for zs in early_z for z in zs])
        done = finish_early(
            *early_z[d - 1], table_e[d - 1 : d], row_factors_e, arrived, (b - a) * rows, parts, head, part
        )
        for (i, j), x in zip(parts, done):
            jobs.append((x, recv_slot, i, j - i, here))
            jobs.append((pass_on(x), recv_slot, i, j - i, there))
        if j < b:
            others = arrived[(j - a) * rows : (b - a) * rows]
            next_jobs.append((others, recv_slot, j, b - j, here))
            last_jobs.append((pass_on(others), recv_slot, j, b - j, there))
    out = place(out, jobs)
    for d in offsets:
        here, there = source_of(me, d), source_of(twin, d)
        arrived = gate(chunks[1][d - 1], out)
        next_jobs.append((arrived, recv_slot, c, end - c, here))
        last_jobs.append((pass_on(arrived), recv_slot, c, end - c, there))
    return covariance, place(place(out, next_jobs), last_jobs)


def shards(increment, vert_rate, zonal_rate, merid_rate, lat_band, slab_owner):
    slabs = increment.shape[0]
    groups = lax.axis_size("tx")
    capacity = 2 * slabs // groups
    rows = increment.shape[1]
    part = rows // 2 if rows % 16 == 0 else rows
    early, head = 15 * capacity // 16, max(3 * capacity // 16, 1) * (rows // part)
    most = max(2 * capacity, head + LEV)
    ladder = sorted({-(-capacity * 21 // 16), -(-capacity * 22 // 16), most})
    lists, v, first_sent, rest_sent = vertical_first(
        increment, vert_rate, slab_owner, groups // CORES, capacity, early, head, part, ladder
    )
    return lax.switch(
        lists[-1][0],
        [functools.partial(run, amount, early, head, part, most) for amount in ladder],
        increment,
        vert_rate,
        zonal_rate,
        merid_rate,
        lat_band,
        slab_owner,
        lists,
        v,
        first_sent,
        rest_sent,
    )


def solution(mesh):
    return jax.shard_map(
        shards,
        mesh=mesh,
        in_specs=(P(None, "ty", "tx"), P(), P(), P(), P(), P()),
        out_specs=(P(None, "ty", "tx"), P("tx", "ty", None)),
        check_vma=False,
    )
```

```python
import functools

import jax
import jax.numpy as jnp
from jax import lax
from jax.experimental import pallas as pl
from jax.experimental.pallas import tpu as pltpu
from jax.sharding import PartitionSpec as P

LEV = 16
VAR = 2
NBANDS = 16
CORES = 2
GROUP = 8
HIGHEST = lax.Precision.HIGHEST
VMEM_LIMIT = 48 * 1024 * 1024
SMEM = pl.BlockSpec(memory_space=pltpu.SMEM)
ANY = pl.BlockSpec(memory_space=pl.ANY)


def call(kernel, name, **how):
    return pl.pallas_call(
        kernel,
        compiler_params=pltpu.CompilerParams(vmem_limit_bytes=VMEM_LIMIT),
        cost_estimate=pl.CostEstimate(flops=0, bytes_accessed=4096, transcendentals=0),
        name=name,
        **how,
    )


def f32(*shape):
    return jax.ShapeDtypeStruct(shape, jnp.float32)


def i32(*shape):
    return jax.ShapeDtypeStruct(shape, jnp.int32)


def gain_of(rates):
    return jnp.sqrt(rates * (2.0 - rates))


def halves(x):
    high = x.astype(jnp.bfloat16)
    low = (x - high.astype(jnp.float32)).astype(jnp.bfloat16)
    return high, low


def exact_dot(a, b):
    return jnp.dot(a, b, precision=HIGHEST, preferred_element_type=jnp.float32)


def iota(shape, dim):
    return lax.broadcasted_iota(jnp.int32, shape, dim)


def select(table, band, shape):
    out = jnp.zeros(shape, jnp.float32)
    for b in range(NBANDS):
        entry = table[b : b + 1, :] if band.shape[1] == 1 else table[:, b : b + 1]
        out = jnp.where(band == b, entry, out)
    return out


def filter_levels(decay, gain, src_ref, dst_ref, rows, cut):
    state, held = None, []
    for level in range(LEV):
        piece = gain[level] * src_ref[level, rows, cut]
        state = piece if state is None else decay[level] * state + piece
        held.append(state)
    state = None
    for level in reversed(range(LEV)):
        piece = gain[level] * held[level]
        state = piece if state is None else decay[level] * state + piece
        dst_ref[level, rows, cut] = state


def level_factors(rate_ref, var):
    rates = [rate_ref[var, level] for level in range(LEV)]
    decay = [1.0 - rate for rate in rates]
    gain = [jnp.sqrt(jnp.full((8, 128), rate * (2.0 - rate), jnp.float32))[:1, :1] for rate in rates]
    return decay, gain


def column_cuts(columns):
    width = 384 if columns % 384 == 0 else 128
    return [slice(start, start + width) for start in range(0, columns, width)]


def write_lists(chips, capacity, head, ladder, owner_ref, send_ref, recv_ref, slot_ref, held_ref, rank_ref, place_ref, step_ref, counts):
    slabs = owner_ref.shape[0]
    most = ladder[-1]
    me = lax.axis_index("tx")
    chip = lax.div(me, CORES)
    for c in range(chips * (1 + CORES)):
        counts[c] = 0
    for e in range((chips - 1) * most):
        send_ref[e] = 0
    for e in range(most):
        recv_ref[e] = 0
        slot_ref[e] = -1
    for e in range(capacity):
        held_ref[e] = -1

    def one(s, _):
        owner = owner_ref[s]
        its_chip = lax.div(owner, CORES)
        rank = counts[its_chip]
        slot = counts[chips + owner]
        counts[its_chip] = rank + 1
        counts[chips + owner] = slot + 1
        rank_ref[s] = rank
        place_ref[s] = slot
        away = lax.rem(its_chip + chips - chip, chips)
        send_ref[jnp.where(away == 0, (chips - 1) * most, (away - 1) * most + rank)] = s
        here = jnp.where(away == 0, rank, most)
        mine = owner == me
        recv_ref[here] = s
        slot_ref[here] = jnp.where(mine, slot, -1)
        held_ref[jnp.where(mine, slot, capacity)] = slot
        return 0

    lax.fori_loop(0, LEV, one, 0, unroll=4)
    for c in range(chips):
        counts[c] = jnp.maximum(counts[c], head)
    lax.fori_loop(LEV, slabs, one, 0, unroll=4)
    needed = counts[0]
    for c in range(1, chips):
        needed = jnp.maximum(needed, counts[c])
    step = jnp.int32(0)
    for amount in ladder[:-1]:
        step = step + jnp.where(needed > amount, 1, 0)
    step_ref[0] = step


def first_rows(e, part):
    return e * part


def rest_row(e, row, rows, part, head):
    return e * (rows - part) + row - part if e < head else head * (rows - part) + (e - head) * rows + row


def filter_block(rate_ref, var, x_ref, v_ref):
    decay, gain = level_factors(rate_ref, var)

    def eight(i, _):
        now = pl.ds(pl.multiple_of(i * 8, 8), 8)
        for cut in column_cuts(x_ref.shape[-1]):
            filter_levels(decay, gain, x_ref, v_ref, now, cut)
        return 0

    lax.fori_loop(0, x_ref.shape[1] // 8, eight, 0)


def first_kernel(chips, capacity, early, head, ladder, rows, part, rate_ref, owner_ref, x_ref, *rest):
    lists, v_ref, first_refs, rest_refs = rest[:7], rest[7], rest[8 : 7 + chips], rest[7 + chips : 6 + 2 * chips]
    counts, x, v, arrive, leave, sem = rest[-6:]
    slices = [pl.ds(at, 8) for at in range(0, part, 8)]
    var = pl.ds(0, LEV)
    reads = [pltpu.make_async_copy(x_ref.at[var, now], x.at[:, now], arrive.at[i]) for i, now in enumerate(slices)]
    writes = [pltpu.make_async_copy(v.at[:, now], v_ref.at[var, now], leave.at[i]) for i, now in enumerate(slices)]
    for copy in reads:
        copy.start()
    write_lists(chips, capacity, head, ladder, owner_ref, *lists, counts)
    decay, gain = level_factors(rate_ref, 0)
    for now, read, write in zip(slices, reads, writes):
        read.wait()
        for cut in column_cuts(x.shape[-1]):
            filter_levels(decay, gain, x, v, now, cut)
        write.start()
    for wait in (False, True):
        for d in range(chips - 1):
            for e in range(early):
                slab = lists[0][d * ladder[-1] + e]
                if e < head:
                    to = first_refs[d].at[pl.ds(first_rows(e, part), part)]
                else:
                    to = rest_refs[d].at[pl.ds(rest_row(e, 0, rows, part, head), part)]

                @pl.when(slab < LEV)
                def _():
                    copy = pltpu.make_async_copy(v.at[slab], to, sem.at[d, e])
                    copy.wait() if wait else copy.start()

    for copy in writes:
        copy.wait()


def second_kernel(chips, most, early, head, rows, rate_ref, x_ref, send_ref, *rest):
    v_ref, rest_refs, sem = rest[chips], rest[1 + chips : 2 * chips], rest[-1]
    part = x_ref.shape[1]
    parts = rows // part
    step, steps = pl.program_id(0), pl.num_programs(0)
    filter_block(rate_ref, lax.div(step + 1, parts), x_ref, v_ref)

    def copies(step, wait):
        var, which = lax.div(step + 1, parts), lax.rem(step + 1, parts)
        for d in range(chips - 1):
            for e in range(early):
                slab = send_ref[d * most + e]
                wanted = lax.div(slab, LEV) == var
                row = rest_row(e, 0, rows, part, head) + which * part
                if e < head:
                    wanted = jnp.logical_and(wanted, which > 0)

                @pl.when(wanted)
                def _():
                    to = rest_refs[d].at[pl.ds(pl.multiple_of(row, 8), part)]
                    copy = pltpu.make_async_copy(v_ref.at[lax.rem(slab, LEV)], to, sem.at[step, d, e])
                    copy.wait() if wait else copy.start()

    copies(step, False)

    @pl.when(step > 0)
    def _():
        copies(step - 1, True)

    @pl.when(step == steps - 1)
    def _():
        copies(step, True)


def vertical_first(increment, vert_rate, slab_owner, chips, capacity, early, head, part, ladder):
    slabs, rows, columns = increment.shape
    most = ladder[-1]
    lists = [(chips - 1) * most + 1, most + 1, most + 1, capacity + 1, slabs, slabs, 1]
    rest_rows = head * (rows - part) + (early - head) * rows
    outs = call(
        functools.partial(first_kernel, chips, capacity, early, head, ladder, rows, part),
        "vertical_first",
        in_specs=[SMEM, SMEM, ANY],
        out_specs=[SMEM] * 7 + [ANY] * (2 * chips - 1),
        out_shape=[i32(n) for n in lists]
        + [f32(*increment.shape)]
        + [f32(head * part, columns)] * (chips - 1)
        + [f32(rest_rows, columns)] * (chips - 1),
        scratch_shapes=[
            pltpu.SMEM((chips * (1 + CORES),), jnp.int32),
            pltpu.VMEM((LEV, part, columns), jnp.float32),
            pltpu.VMEM((LEV, part, columns), jnp.float32),
            pltpu.SemaphoreType.DMA((part // 8,)),
            pltpu.SemaphoreType.DMA((part // 8,)),
            pltpu.SemaphoreType.DMA((chips - 1, early)),
        ],
    )(vert_rate, slab_owner, increment)
    return outs[:7], outs[7], outs[8 : 7 + chips], outs[7 + chips :]


def vertical_second(increment, vert_rate, send, v, rest_sent, early, head, part, most):
    slabs, rows, columns = increment.shape
    chips = 1 + len(rest_sent)
    parts = rows // part
    steps = VAR * parts - 1
    spec = pl.BlockSpec((LEV, part, columns), lambda n: (lax.div(n + 1, parts), lax.rem(n + 1, parts), 0))
    outs = call(
        functools.partial(second_kernel, chips, most, early, head, rows),
        "vertical_second",
        grid=(steps,),
        in_specs=[SMEM, spec, SMEM] + [ANY] * chips,
        out_specs=[spec] + [ANY] * (chips - 1),
        out_shape=[f32(*v.shape)] + [f32(*a.shape) for a in rest_sent],
        scratch_shapes=[pltpu.SemaphoreType.DMA((steps, chips - 1, early))],
        input_output_aliases={3 + n: n for n in range(chips)},
    )(vert_rate, increment, send, v, *rest_sent)
    return outs[0], outs[1:]


def ends_kernel(band_ref, zonal_ref, v_ref, ends_ref, la_ref):
    levels, rows, columns = v_ref.shape
    var = pl.program_id(0)

    @pl.when(var == 0)
    def _():
        first = lax.axis_index("ty") * rows

        def fetch(r, _):
            la_ref[pl.ds(r, 1), :] = zonal_ref[pl.ds(band_ref[first + r], 1), :]
            return 0

        lax.fori_loop(0, rows, fetch, 0)
        la_ref[...] = jnp.log1p(-la_ref[...])
        ends_ref[...] = jnp.zeros(ends_ref.shape, jnp.float32)

    lane = iota((1, 128), 1).astype(jnp.float32)
    slabs = la_ref.shape[1]
    slab_lane = iota((8, slabs), 1)
    blocks = columns // 128

    def row_sums(parts):
        high, low = halves(jnp.concatenate(parts, axis=0))
        ones = jnp.ones((128, 128), jnp.bfloat16)
        dot = functools.partial(jnp.dot, preferred_element_type=jnp.float32)
        return dot(high, ones) + dot(low, ones)

    def eight(i, _):
        now = pl.ds(pl.multiple_of(i * 8, 8), 8)
        la_rows = jnp.where(var == 1, la_ref[now, LEV:], la_ref[now, :LEV])
        whole_rows = jnp.exp(la_rows * 128.0)
        rights, lefts = [], []
        for level in range(levels):
            la = jnp.broadcast_to(la_rows[:, level : level + 1], (8, 128))
            whole = jnp.broadcast_to(whole_rows[:, level : level + 1], (8, 128))
            pieces = [v_ref[level, now, b * 128 : (b + 1) * 128] for b in range(blocks)]
            right, left = pieces[0], pieces[-1]
            for b in range(1, blocks):
                right = whole * right + pieces[b]
                left = whole * left + pieces[blocks - 1 - b]
            rights.append(right * jnp.exp(la * (127.0 - lane)))
            lefts.append(left * jnp.exp(la * lane))
        right, left = row_sums(rights), row_sums(lefts)
        right_ends, left_ends = ends_ref[0, now, :], ends_ref[1, now, :]
        for level in range(levels):
            here = slab_lane == var * LEV + level
            right_ends = jnp.where(here, right[level * 8 : (level + 1) * 8, :slabs], right_ends)
            left_ends = jnp.where(here, left[level * 8 : (level + 1) * 8, :slabs], left_ends)
        ends_ref[0, now, :] = right_ends
        ends_ref[1, now, :] = left_ends
        return 0

    lax.fori_loop(0, rows // 8, eight, 0, unroll=2 if rows % 16 == 0 else 1)


def zonal_ends(v, zonal_rate, lat_band):
    slabs, rows, columns = v.shape
    return call(
        ends_kernel,
        "ends",
        grid=(VAR,),
        in_specs=[
            SMEM,
            pl.BlockSpec(zonal_rate.shape, lambda v: (0, 0)),
            pl.BlockSpec((LEV, rows, columns), lambda v: (v, 0, 0)),
        ],
        out_specs=pl.BlockSpec((2, rows, slabs), lambda v: (0, 0, 0)),
        out_shape=f32(2, rows, slabs),
        scratch_shapes=[pltpu.VMEM((rows, slabs), jnp.float32)],
    )(lat_band, zonal_rate, v)


def gate_kernel(*refs):
    pass


def gate(value, *after):
    return call(
        gate_kernel,
        "gate",
        in_specs=[ANY] * (1 + len(after)),
        out_specs=ANY,
        out_shape=jax.ShapeDtypeStruct(value.shape, value.dtype),
        input_output_aliases={0: 0},
    )(value, *after)


def gate_all(values, *after):
    return call(
        gate_kernel,
        "gate_all",
        in_specs=[ANY] * (len(values) + len(after)),
        out_specs=[ANY] * len(values),
        out_shape=[jax.ShapeDtypeStruct(value.shape, value.dtype) for value in values],
        input_output_aliases={n: n for n in range(len(values))},
    )(*values, *after)


COLUMNS = 8


def tables_kernel(chips, devices, early, width, recv_ref, zonal_ref, merid_ref, merid_t_ref, band_ref, own_band_ref, row_ref, *rest):
    own_ends, twin_ends = rest[:chips], rest[chips : 2 * chips]
    t_ref, te_ref, r_ref, re_ref, coef_ref, hold = rest[2 * chips :]
    rows, slabs = own_ends[0].shape[1:]
    groups = chips * CORES
    me, place_y = lax.axis_index("tx"), lax.axis_index("ty")

    k, m = iota((rows, rows), 0), iota((rows, rows), 1)
    below, above = (k >= m).astype(jnp.float32), (k <= m).astype(jnp.float32)
    own_band = own_band_ref[...]
    la = jnp.log1p(-select(zonal_ref[...], own_band, (rows, slabs)))

    def tables_of(rates):
        log_decay = jnp.log1p(-rates)
        inclusive = exact_dot(below, log_decay)
        exclusive = inclusive - log_decay
        gains = gain_of(rates)
        sums = exact_dot(above, gains * jnp.exp(inclusive + exclusive))
        return inclusive, exclusive, gains, sums

    inclusive, exclusive, gains, sums = tables_of(select(merid_ref[...], own_band, (rows, slabs)))
    whole = jnp.exp(inclusive[rows - 1 :, :])
    before = gains * jnp.exp(-inclusive)
    after = jnp.exp(-exclusive)
    meridional = [whole * before, before * sums, after * sums, after, whole * after]

    tile_decay = jnp.exp(la * float(width))
    my_chip, my_core = lax.div(me, CORES), lax.rem(me, CORES)

    def ends_of(t, side):
        away = lax.rem(my_chip + chips - t // CORES, chips)
        out = jnp.zeros((rows, slabs), jnp.float32)
        for d in range(chips):
            value = jnp.where(my_core == t % CORES, own_ends[d][side], twin_ends[d][side])
            out = jnp.where(away == d, value, out)
        return out

    from_left = [jnp.zeros((rows, slabs), jnp.float32)]
    for t in range(groups):
        from_left.append(ends_of(t, 0) + tile_decay * from_left[-1])
    from_right = [-jnp.exp(la) * from_left[-1]]
    for t in reversed(range(1, groups)):
        from_right.append(ends_of(t, 1) + tile_decay * from_right[-1])
    from_right = from_right[::-1]

    def entering(tile):
        left = right = jnp.zeros((rows, slabs), jnp.float32)
        for t in range(groups):
            left = jnp.where(tile == t, from_left[t], left)
            right = jnp.where(tile == t, from_right[t], right)
        return left, right

    for c, table in enumerate([la, *entering(me), *meridional]):
        for g in range(slabs // GROUP):
            t_ref[g, c] = table[:, g * GROUP : (g + 1) * GROUP]
    slab, entry = iota((slabs, early), 0), iota((slabs, early), 1)
    hit = jnp.zeros((slabs, early), jnp.float32)
    for e in range(early):
        hit = jnp.where(jnp.logical_and(entry == e, slab == recv_ref[e]), 1.0, hit)
    common = [exact_dot(table, hit) for table in [la, *meridional]]
    for d in range(1, chips):
        left, right = entering(lax.rem(me + groups - CORES * d, groups))
        for c, table in enumerate([common[0], exact_dot(left, hit), exact_dot(right, hit), *common[1:]]):
            te_ref[d - 1, c] = table

    wide = 3 * rows
    k, m = iota((rows, wide), 0), iota((rows, wide), 1)
    m = m - jnp.where(m >= 2 * rows, 2 * rows, jnp.where(m >= rows, rows, 0))
    upto, onward = (k <= m).astype(jnp.float32), (k >= m).astype(jnp.float32)
    band_row = row_ref[...]
    rates = select(merid_t_ref[...], band_row, (slabs, wide))
    log_row = jnp.log1p(-rates[:, :rows])
    inclusive_row = exact_dot(log_row, upto)
    here = inclusive_row[:, :rows]
    sums_row = exact_dot(gain_of(rates[:, :rows]) * jnp.exp(2.0 * here - log_row), onward)
    before_row = gain_of(rates) * jnp.exp(-inclusive_row)
    after_row = before_row * sums_row
    for s in range(slabs):
        r_ref[s, 0:1] = before_row[s : s + 1]
        r_ref[s, 1:2] = after_row[s : s + 1]
    for e in range(early):
        re_ref[e] = r_ref[recv_ref[e]]

    decay, cross = [], []
    for n in range(devices):
        band = band_ref[n * rows : (n + 1) * rows]
        inclusive, _, _, sums = tables_of(select(merid_ref[...], band, (rows, slabs)))
        decay.append(jnp.exp(inclusive[rows - 1 :, :]))
        cross.append(sums[0:1, :])
    decay, cross = jnp.concatenate(decay, axis=0), jnp.concatenate(cross, axis=0)
    device = iota((devices, slabs), 0)
    own_f, own_bf, own_b = jnp.ones_like(decay), jnp.zeros_like(decay), jnp.ones_like(decay)
    stage, bit = 0, 1
    while bit < devices:
        upper = lax.rem(lax.div(device, bit), 2) == 1
        swap = lambda a: jnp.concatenate([a[n ^ bit : (n ^ bit) + 1] for n in range(devices)], axis=0)
        other_decay, other_cross = swap(decay), swap(cross)
        d_low, d_high = jnp.where(upper, other_decay, decay), jnp.where(upper, decay, other_decay)
        c_low, c_high = jnp.where(upper, other_cross, cross), jnp.where(upper, cross, other_cross)
        for c, table in enumerate([d_low, d_high, c_high, own_f, own_bf, own_b]):
            hold[...] = table
            coef_ref[stage, c : c + 1] = hold[pl.ds(place_y, 1), :]
        own_bf = jnp.where(upper, own_bf * d_low, own_bf + own_b * c_high * d_low)
        own_f = jnp.where(upper, own_f * d_low, own_f)
        own_b = jnp.where(upper, own_b, own_b * d_high)
        decay, cross = d_low * d_high, c_low + d_low * d_low * c_high
        stage, bit = stage + 1, 2 * bit


def tables(zonal_rate, merid_rate, lat_band, recv_slab, own_ends, twin_ends, columns, early):
    chips = len(own_ends)
    devices = lax.axis_size("ty")
    _, rows, slabs = own_ends[0].shape
    stages = (devices - 1).bit_length()
    own = lax.dynamic_slice_in_dim(lat_band, lax.axis_index("ty") * rows, rows)
    vmem = pl.BlockSpec(memory_space=pltpu.VMEM)
    return call(
        functools.partial(tables_kernel, chips, devices, early, columns),
        "tables",
        in_specs=[SMEM] + [vmem] * (6 + 2 * chips),
        out_specs=[vmem] * 5,
        out_shape=[
            f32(slabs // GROUP, COLUMNS, rows, GROUP),
            f32(chips - 1, COLUMNS, rows, early),
            f32(slabs, 2, 3 * rows),
            f32(early, 2, 3 * rows),
            f32(stages, 6, slabs),
        ],
        scratch_shapes=[pltpu.VMEM((devices, slabs), jnp.float32)],
    )(
        recv_slab,
        zonal_rate,
        merid_rate,
        merid_rate.T,
        lat_band[:, None],
        own[:, None],
        jnp.tile(own, 3)[None, :],
        *own_ends,
        *twin_ends,
    )


def zonal_tile(v, la, left, right, block):
    rows, columns = v.shape
    half = block // 2
    blocks = columns // block
    j, i = iota((block, block), 0), iota((block, block), 1)
    upto = jnp.where(j <= i, 1.0, 0.0).astype(jnp.bfloat16)
    onward = jnp.where(j >= i, 1.0, 0.0).astype(jnp.bfloat16)
    power = la * (iota((1, block), 1) - half).astype(jnp.float32)
    up, down = jnp.exp(power), jnp.exp(-power)
    value = [v[:, b * block : (b + 1) * block] for b in range(blocks)]

    def totals(scale, ones):
        high, low = halves(jnp.concatenate([x * scale for x in value], axis=0))
        dot = functools.partial(jnp.dot, preferred_element_type=jnp.float32)
        total = dot(high, ones) + dot(low, ones)
        return [total[b * rows : (b + 1) * rows] for b in range(blocks)]

    enter = jnp.exp(la * (half + 1.0))
    state, rising = left, []
    for total in totals(down, upto):
        now = up * (total + enter * state)
        state = now[:, block - 1 :]
        rising.append(now)
    enter = jnp.exp(la * float(half))
    state, result = right, [None] * blocks
    parts = totals(up, onward)
    for b in reversed(range(blocks)):
        now = down * (parts[b] + enter * state)
        state = now[:, :1]
        result[b] = rising[b] + now - value[b]
    return result


def zonal_kernel(v_ref, t_ref, z_ref, o_ref):
    for s in range(v_ref.shape[0]):
        block = 256 if v_ref.shape[-1] % 256 == 0 else 128
        column = lambda c: jnp.broadcast_to(t_ref[0, c, :, s : s + 1], (t_ref.shape[2], block))
        result = zonal_tile(v_ref[s], column(0), column(1), column(2), block)
        for side in range(2):
            weight = column(3 + side)
            for b, z in enumerate(result):
                o_ref[side, s : s + 1, b * block : (b + 1) * block] = jnp.sum(z * weight, axis=0, keepdims=True)
        for b, z in enumerate(result):
            z_ref[s, :, b * block : (b + 1) * block] = z


def zonal(v, table):
    slabs, rows, columns = v.shape
    return call(
        zonal_kernel,
        "zonal",
        grid=(slabs // GROUP,),
        in_specs=[
            pl.BlockSpec((GROUP, rows, columns), lambda s: (s, 0, 0)),
            pl.BlockSpec((1, *table.shape[1:]), lambda s: (s, 0, 0, 0)),
        ],
        out_specs=[
            pl.BlockSpec((GROUP, rows, columns), lambda s: (s, 0, 0)),
            pl.BlockSpec((2, GROUP, columns), lambda s: (0, s, 0)),
        ],
        out_shape=[f32(*v.shape), f32(2, slabs, columns)],
    )(v, table)


def zonal_rows_kernel(pieces, v_ref, t_ref, z_ref):
    block = 256 if v_ref.shape[-1] % 256 == 0 else 128
    for at, e, row, count in pieces:
        column = lambda c: jnp.broadcast_to(t_ref[0, c, row : row + count, e : e + 1], (count, block))
        result = zonal_tile(v_ref[at : at + count], column(0), column(1), column(2), block)
        for b, z in enumerate(result):
            z_ref[at : at + count, b * block : (b + 1) * block] = z


def zonal_rows(v, table, pieces):
    vmem = pl.BlockSpec(memory_space=pltpu.VMEM)
    return call(
        functools.partial(zonal_rows_kernel, pieces),
        "zonal_rows",
        in_specs=[vmem, vmem],
        out_specs=vmem,
        out_shape=f32(*v.shape),
    )(v, table)


def finish_tile(z, column, row_factors, f_in, b_in):
    rows = z.shape[0]
    wide = 3 * rows
    i, r = iota((rows, wide), 0), iota((rows, wide), 1)
    third = r >= 2 * rows
    r = r - jnp.where(third, 2 * rows, jnp.where(r >= rows, rows, 0))
    a, c = column(5), column(6)
    matrix = jnp.where(i >= r, a * row_factors[0:1], c * row_factors[1:2])
    high = matrix.astype(jnp.bfloat16)
    low = (matrix - high.astype(jnp.float32)).astype(jnp.bfloat16)
    matrix = jnp.where(third, low.astype(jnp.float32), high.astype(jnp.float32)).astype(jnp.bfloat16)
    z_high, z_low = halves(z)
    dot = functools.partial(jnp.dot, preferred_element_type=jnp.float32)
    if rows % 16 == 0:
        result = dot(matrix, jnp.concatenate([z_high, z_low, z_high], axis=0))
    else:
        result = dot(matrix[:, :rows], z_high) + dot(matrix[:, rows : 2 * rows], z_low)
        result = result + dot(matrix[:, 2 * rows :], z_high)
    return result + a * f_in + column(7) * b_in


def finish_kernel(chips, capacity, bounds, twin_bounds, rate_ref, owner_ref, rank_ref, place_ref, held_ref, z_ref, t_ref, r_ref, s_ref, *rest):
    cov_ref = rest[0]
    chunk_refs = [rest[1 + k * (chips - 1) : 1 + (k + 1) * (chips - 1)] for k in range(len(bounds))]
    rest = rest[1 + len(bounds) * (chips - 1) :]
    twin_refs, rest = rest[: len(twin_bounds)], rest[len(twin_bounds) :]
    out_ref, smooth, blank, early_states, sem, wipe_sem, state_sem = rest
    early = bounds[0][0]
    levels, rows, columns = z_ref.shape
    var = pl.program_id(0)
    me = lax.axis_index("tx")
    my_chip = lax.div(me, CORES)
    first = pl.multiple_of(me * columns, 128)

    def wipe(wait):
        for e in range(capacity):

            @pl.when(jnp.logical_and(var == 0, held_ref[e] < 0))
            def _():
                copy = pltpu.make_async_copy(blank, out_ref.at[e], wipe_sem.at[e])
                copy.wait() if wait else copy.start()

    @pl.when(var == 0)
    def _():
        blank[...] = jnp.zeros(blank.shape, jnp.float32)
        early_states[...] = jnp.zeros(early_states.shape, jnp.float32)

    wipe(False)

    def deliver(level, wait):
        slab = var * LEV + level
        owner, rank, slot = owner_ref[slab], rank_ref[slab], place_ref[slab]
        away = lax.rem(lax.div(owner, CORES) + chips - my_chip, chips)

        def move(condition, to):
            @pl.when(condition)
            def _():
                copy = pltpu.make_async_copy(smooth.at[level], to(), sem.at[level])
                copy.wait() if wait else copy.start()

        for d in range(1, chips):
            there = away == d
            for (a, b), refs in zip(bounds, chunk_refs):
                within = jnp.logical_and(there, jnp.logical_and(rank >= a, rank < b))
                at = pl.multiple_of((rank - a) * rows, 8)
                move(within, lambda: refs[d - 1].at[pl.ds(at, rows)])
            if not wait:

                @pl.when(jnp.logical_and(there, rank < early))
                def _():
                    early_states[d - 1, pl.ds(rank, 1), :] = s_ref[0, level : level + 1, :]
                    early_states[d - 1, pl.ds(early + rank, 1), :] = s_ref[1, level : level + 1, :]
        move(owner == me, lambda: out_ref.at[slot, :, pl.ds(first, columns)])
        for (a, b), ref in zip(twin_bounds, twin_refs):
            within = jnp.logical_and(slot >= a, slot < b)
            at = pl.multiple_of((slot - a) * rows, 8)
            move(jnp.logical_and(jnp.logical_and(away == 0, owner != me), within), lambda: ref.at[pl.ds(at, rows)])

    for level in range(levels):
        column = lambda c: t_ref[level // GROUP, c, :, level % GROUP : level % GROUP + 1]
        states = s_ref[:, level, :]
        smooth[level] = finish_tile(z_ref[level], column, r_ref[level], states[0:1], states[1:2])
        deliver(level, False)

    def send_states(wait):
        for d in range(1, chips):

            @pl.when(var == VAR - 1)
            def _():
                to = chunk_refs[0][d - 1].at[pl.ds((bounds[0][1] - early) * rows, early_states.shape[1])]
                copy = pltpu.make_async_copy(early_states.at[d - 1], to, state_sem.at[d - 1])
                copy.wait() if wait else copy.start()

    send_states(False)
    decay, gain = level_factors(rate_ref, var)

    def eight(i, _):
        now = pl.ds(pl.multiple_of(i * 8, 8), 8)
        for cut in column_cuts(columns):
            filter_levels(decay, gain, smooth, cov_ref, now, cut)
        return 0

    lax.fori_loop(0, rows // 8, eight, 0)
    for level in range(levels):
        deliver(level, True)
    send_states(True)
    wipe(True)


def finish(z, vert_rate, owner, rank, place_of, held, table, row_factors, states, chips, capacity, bounds, twin_bounds):
    slabs, rows, columns = z.shape
    early = bounds[0][0]
    state_rows = -(-2 * early // 8) * 8
    chunks = [f32((b - a) * rows + (state_rows if a == early else 0), columns) for a, b in bounds]
    outs = call(
        functools.partial(finish_kernel, chips, capacity, bounds, twin_bounds),
        "finish",
        grid=(VAR,),
        in_specs=[SMEM] * 5
        + [
            pl.BlockSpec((LEV, rows, columns), lambda v: (v, 0, 0)),
            pl.BlockSpec((LEV // GROUP, COLUMNS, rows, GROUP), lambda v: (v, 0, 0, 0)),
            pl.BlockSpec((LEV, 2, 3 * rows), lambda v: (v, 0, 0)),
            pl.BlockSpec((2, LEV, columns), lambda v: (0, v, 0)),
        ],
        out_specs=[pl.BlockSpec((LEV, rows, columns), lambda v: (v, 0, 0))]
        + [ANY] * (1 + len(twin_bounds) + len(bounds) * (chips - 1)),
        out_shape=[f32(*z.shape)]
        + [chunk for chunk in chunks for _ in range(chips - 1)]
        + [f32((b - a) * rows, columns) for a, b in twin_bounds]
        + [f32(capacity, rows, chips * CORES * columns)],
        scratch_shapes=[
            pltpu.VMEM((LEV, rows, columns), jnp.float32),
            pltpu.VMEM((rows, chips * CORES * columns), jnp.float32),
            pltpu.VMEM((chips - 1, state_rows, columns), jnp.float32),
            pltpu.SemaphoreType.DMA((LEV,)),
            pltpu.SemaphoreType.DMA((capacity,)),
            pltpu.SemaphoreType.DMA((chips - 1,)),
        ],
    )(vert_rate, owner, rank, place_of, held, z, table, row_factors, states)
    sent = [outs[1 + k * (chips - 1) : 1 + (k + 1) * (chips - 1)] for k in range(len(bounds))]
    return outs[0], sent, outs[1 + len(bounds) * (chips - 1) : -1], outs[-1]


def finish_early_kernel(first_state, early, head, part, rows, t_ref, r_ref, s_ref, first_ref, rest_ref, *done_refs):
    e = 0
    for done_ref in done_refs:
        for at in range(0, done_ref.shape[0], rows):
            if e >= early:
                done_ref[at : at + rows] = s_ref[(e - early) * rows : (e - early + 1) * rows]
                e += 1
                continue
            column = lambda c: t_ref[0, c, :, e : e + 1]
            f_in = s_ref[first_state + e : first_state + e + 1]
            b_in = s_ref[first_state + early + e : first_state + early + e + 1]
            if e >= head:
                row = rest_row(e, 0, rows, part, head)
                z = rest_ref[row : row + rows]
            else:
                z = first_ref[first_rows(e, part) : first_rows(e, part) + part]
                if part < rows:
                    row = rest_row(e, part, rows, part, head)
                    z = jnp.concatenate([z, rest_ref[row : row + rows - part]], axis=0)
            done_ref[at : at + rows] = finish_tile(z, column, r_ref[e], f_in, b_in)
            e += 1


def finish_early(first_z, rest_z, table, row_factors, states, first_state, parts, head, part):
    rows, early = table.shape[2:]
    vmem = pl.BlockSpec(memory_space=pltpu.VMEM)
    return call(
        functools.partial(finish_early_kernel, first_state, early, head, part, rows),
        "finish_early",
        in_specs=[vmem] * 5,
        out_specs=[vmem] * len(parts),
        out_shape=[f32((b - a) * rows, states.shape[1]) for a, b in parts],
    )(table, row_factors, states, first_z, rest_z)


def place_kernel(jobs, tile_ref, *rest):
    slots = rest[: len(jobs)]
    srcs = rest[len(jobs) : 2 * len(jobs)]
    out_ref, held, arrive, leave = rest[-4:]
    rows, columns = held.shape[-2:]
    entries, n = [], 0
    for k, (first, count) in enumerate(jobs):
        for e in range(count):
            entries.append((k, e, first + e, n))
            n += 1

    def read(k, e, at, n):
        return pltpu.make_async_copy(srcs[k].at[pl.ds(e * rows, rows)], held.at[n], arrive.at[n])

    def write(k, e, at, n):
        start = pl.multiple_of(tile_ref[k] * columns, 128)
        return pltpu.make_async_copy(held.at[n], out_ref.at[slots[k][at], :, pl.ds(start, columns)], leave.at[n])

    def each(act):
        for k, e, at, n in entries:

            @pl.when(slots[k][at] >= 0)
            def _():
                act(k, e, at, n)

    def onward(*job):
        read(*job).wait()
        write(*job).start()

    each(lambda *job: read(*job).start())
    each(onward)
    each(lambda *job: write(*job).wait())


def place(out, jobs):
    n = sum(job[3] for job in jobs)
    count = len(jobs)
    return call(
        functools.partial(place_kernel, [(job[2], job[3]) for job in jobs]),
        "place",
        in_specs=[SMEM] * (1 + count) + [ANY] * (count + 1),
        out_specs=ANY,
        out_shape=f32(*out.shape),
        scratch_shapes=[
            pltpu.VMEM((n, out.shape[1], jobs[0][0].shape[1]), jnp.float32),
            pltpu.SemaphoreType.DMA((n,)),
            pltpu.SemaphoreType.DMA((n,)),
        ],
        input_output_aliases={1 + 2 * count: 0},
    )(jnp.stack([job[4] for job in jobs]), *[job[1] for job in jobs], *[job[0] for job in jobs], out)


def scan_rows(states, coef):
    count = lax.axis_size("ty")
    place_y = lax.axis_index("ty")
    f_end, b_start = states[0], states[1]
    f_in = b_in = jnp.zeros_like(f_end)
    stage, bit = 0, 1
    while bit < count:
        upper = (place_y // bit) % 2 == 1
        pairs = [(i, i ^ bit) for i in range(count)]
        p_low, p_high, q_high, own_f, own_bf, own_b = [coef[stage, c][:, None] for c in range(6)]
        low = lambda mine, other: jnp.where(upper, other, mine)
        high = lambda mine, other: jnp.where(upper, mine, other)
        if 2 * bit < count:
            both = states if bit == 1 else jnp.stack([f_end, b_start])
            other_f, other_b = lax.ppermute(both, "ty", pairs)
            f_low, f_high = low(f_end, other_f), high(f_end, other_f)
            b_low, b_high = low(b_start, other_b), high(b_start, other_b)
        else:
            other = lax.ppermute(jnp.where(upper, b_start, f_end), "ty", pairs)
            f_low, b_high = low(f_end, other), high(b_start, other)
        from_above = b_high + q_high * f_low
        f_in = f_in + jnp.where(upper, own_f * f_low, 0.0)
        b_in = b_in + jnp.where(upper, own_bf * f_low, own_b * from_above)
        if 2 * bit < count:
            f_end = f_high + p_high * f_low
            b_start = b_low + p_low * from_above
        stage, bit = stage + 1, 2 * bit
    return jnp.stack([f_in, b_in])


def split(first, last, sizes):
    bounds = []
    for size in [*sizes, last]:
        if first < last:
            bounds.append((first, min(first + size, last)))
            first += size
    return bounds


def as_one(ready, function, *operands, otherwise=None):
    shapes = jax.eval_shape(function, *operands)
    empty = lambda *_: jax.tree.map(lambda x: jnp.zeros(x.shape, x.dtype), shapes)
    return lax.cond(ready, function, otherwise or empty, *operands)


def run(amount, early, head, part, most, increment, vert_rate, zonal_rate, merid_rate, lat_band, slab_owner, lists, v, first_sent, rest_sent):
    slabs, rows, columns = v.shape
    groups = lax.axis_size("tx")
    chips = groups // CORES
    capacity = 2 * slabs // groups
    me = lax.axis_index("tx")
    twin = me ^ 1
    twins = [(i, i ^ 1) for i in range(groups)]
    hop = lambda d: [(i, (i + CORES * d) % groups) for i in range(groups)]
    across = lambda values: [lax.ppermute(a, "tx", hop(d + 1)) for d, a in enumerate(values)]
    pass_on = lambda a: lax.ppermute(a, "tx", twins)
    offsets = range(1, chips)
    source_of = lambda who, d: (who + groups - CORES * d) % groups
    send, recv_slab, recv_slot, held, rank, place_of, step = lists
    ready = step[0] >= 0
    bounds = split(early, amount, [max(amount - early - capacity // 4 - 1, 1), amount])
    twin_bounds = split(0, capacity, [capacity // 2] * 2)

    first_v = across(first_sent)
    v, rest_sent = vertical_second(increment, vert_rate, send, v, rest_sent, early, head, part, most)
    ends = zonal_ends(v, zonal_rate, lat_band)
    own_ends = [ends, *across([ends] * (chips - 1))]
    gated = gate_all([*rest_sent, *first_v], *own_ends[1:])
    rest_v, first_v = across(gated[: chips - 1]), gated[chips - 1 :]

    def tile(v, own_ends):
        twin_ends = [pass_on(a) for a in own_ends]
        table, table_e, row_factors, row_factors_e, coef = tables(
            zonal_rate, merid_rate, lat_band, recv_slab, own_ends, twin_ends, columns, early
        )
        z, states = zonal(v, table)
        states = scan_rows(states, coef)
        done = finish(
            z, vert_rate, slab_owner, rank, place_of, held, table, row_factors, states, chips, capacity, bounds, twin_bounds
        )
        return done, table_e, row_factors_e

    (covariance, chunks, twin_sent, out), table_e, row_factors_e = as_one(ready, tile, v, own_ends)
    from_twin = [pass_on(a) for a in twin_sent]
    chunks = [across(sent) for sent in chunks]

    out = place(out, [(x, held, i, j - i, twin) for (i, j), x in zip(twin_bounds, from_twin)])
    parts = split(0, min(capacity, bounds[0][1]), [capacity // 4] * 4)
    first_pieces = [(first_rows(e, part), e, 0, part) for e in range(head)]
    rest_pieces = [(rest_row(e, part, rows, part, head), e, part, rows - part) for e in range(head) if part < rows]
    rest_pieces += [(rest_row(e, 0, rows, part, head), e, 0, rows) for e in range(head, early)]
    early_z, jobs, next_jobs, last_jobs = [], [], [], []
    for d in offsets:
        first_z = zonal_rows(first_v[d - 1], table_e[d - 1 : d], first_pieces)
        early_z.append([first_z, zonal_rows(gate(rest_v[d - 1], first_z, out), table_e[d - 1 : d], rest_pieces)])
    (a, b), (c, end) = bounds
    for d in offsets:
        here, there = source_of(me, d), source_of(twin, d)
        arrived = gate(chunks[0][d - 1], *[z for zs in early_z for z in zs])
        done = finish_early(
            *early_z[d - 1], table_e[d - 1 : d], row_factors_e, arrived, (b - a) * rows, parts, head, part
        )
        for (i, j), x in zip(parts, done):
            jobs.append((x, recv_slot, i, j - i, here))
            jobs.append((pass_on(x), recv_slot, i, j - i, there))
        if j < b:
            others = arrived[(j - a) * rows : (b - a) * rows]
            next_jobs.append((others, recv_slot, j, b - j, here))
            last_jobs.append((pass_on(others), recv_slot, j, b - j, there))
    out = place(out, jobs)
    for d in offsets:
        here, there = source_of(me, d), source_of(twin, d)
        arrived = gate(chunks[1][d - 1], out)
        next_jobs.append((arrived, recv_slot, c, end - c, here))
        last_jobs.append((pass_on(arrived), recv_slot, c, end - c, there))
    return covariance, place(place(out, next_jobs), last_jobs)


def shards(increment, vert_rate, zonal_rate, merid_rate, lat_band, slab_owner):
    slabs = increment.shape[0]
    groups = lax.axis_size("tx")
    capacity = 2 * slabs // groups
    rows = increment.shape[1]
    part = rows // 2 if rows % 16 == 0 else rows
    early, head = 15 * capacity // 16, max(3 * capacity // 16, 1) * (rows // part)
    most = max(2 * capacity, head + LEV)
    ladder = sorted({-(-capacity * 21 // 16), -(-capacity * 22 // 16), most})
    lists, v, first_sent, rest_sent = vertical_first(
        increment, vert_rate, slab_owner, groups // CORES, capacity, early, head, part, ladder
    )
    return lax.switch(
        lists[-1][0],
        [functools.partial(run, amount, early, head, part, most) for amount in ladder],
        increment,
        vert_rate,
        zonal_rate,
        merid_rate,
        lat_band,
        slab_owner,
        lists,
        v,
        first_sent,
        rest_sent,
    )


def solution(mesh):
    return jax.shard_map(
        shards,
        mesh=mesh,
        in_specs=(P(None, "ty", "tx"), P(), P(), P(), P(), P()),
        out_specs=(P(None, "ty", "tx"), P("tx", "ty", None)),
        check_vma=False,
    )
```
